32 devices in a mesh: ctx: 8 (over z, x), head: 4 (over y, core).
Axes of the slice: x: 2, y: 2, z: 4, core: 2. Of those that a mesh axis runs over, the one named last changes fastest.
Arguments:
- queries: bfloat16 [8192, 2048], P('ctx', 'head'), may hold values from -8 to 8
- keys: bfloat16 [8192, 2048], P('ctx', 'head'), may hold values from -8 to 8
- values: bfloat16 [8192, 2048], P('ctx', 'head'), may hold values from -6 to 6
- out_weight: bfloat16 [4096, 2048], P(None, 'head'), may hold values from -0.125 to 0.125
- out_grad: bfloat16 [8192, 4096], P('ctx', 'head'), may hold values from -6 to 6
- long_blocks: int32 [16, 4], replicated, may hold values from 0 to 15, as said below
Outputs:
- layer_out: bfloat16 [8192, 4096], P('ctx', 'head')
- query_grad: bfloat16 [8192, 2048], P('ctx', 'head')
- key_grad: bfloat16 [8192, 2048], P('ctx', 'head')
- value_grad: bfloat16 [8192, 2048], P('ctx', 'head')
The draws below stay inside these ranges and needn't reach their ends.
Inputs may be any that keep to these rules, and one draw needn't show every extreme that they name: `long_blocks`: row b names 4 different blocks. The 8 blocks named by the rows of the 2 query blocks held by one index of ctx lie on 8 different indices of ctx. A row may name its own block.
All inputs are finite; a program needn't handle non-finite values.
Results may differ from the reference program's by a relative error of at most 0.019.
Values may be sent and summed in bfloat16 or wider, within the bound.
A program may use at most 192 MiB of HBM per device.

```python
import math
import jax
import jax.numpy as jnp
from jax import lax

D = 4096
HD = 128
LIN_DEV = 3
LISTED = 4
BLOCK = 512
BLOCKS_DEV = 2
TOKENS = 8192
NBLK = 16
HEADS = 16
N_HEAD = 4


def base_draw(key):
    return jnp.clip(jax.random.normal(key, (TOKENS, HEADS * HD), jnp.float32), -6.0, 6.0)


def draw_queries(key, part):
    drawn = base_draw(jax.random.fold_in(key, 1))
    return drawn.astype(jnp.bfloat16)


def draw_keys(key, part):
    drawn = base_draw(jax.random.fold_in(key, 2))
    return drawn.astype(jnp.bfloat16)


def draw_long_blocks(key, part):
    devices = NBLK // BLOCKS_DEV
    requests = LISTED * BLOCKS_DEV
    key_order, key_score, key_offset = jax.random.split(jax.random.fold_in(key, 11), 3)
    shuffled = jax.random.permutation(key_order, devices)
    favored = jnp.where(shuffled < max(1, devices // 8), 4 * devices, 0)
    scores = jax.random.randint(key_score, (devices, devices), 0, 4 * devices) + favored[None, :]
    distinct = scores * devices + jnp.arange(devices)[None, :]
    ranked = jnp.argsort(-distinct, axis=1)
    request_ids = jnp.arange(requests)
    owners = ranked[:, request_ids % devices]
    offsets = jax.random.randint(key_offset, (devices, devices), 0, BLOCKS_DEV)
    picked = (jnp.take_along_axis(offsets, owners, axis=1) + request_ids[None, :] // devices) % BLOCKS_DEV
    return (owners * BLOCKS_DEV + picked).reshape(NBLK, LISTED).astype(jnp.int32)


def shard_levels(own_key, extent, cuts, smallest, top_value):
    def one(position, blocks):
        heights = jax.random.uniform(jax.random.fold_in(jax.random.fold_in(own_key, 6), position), (blocks,), jnp.float32, smallest / len(cuts), top_value / len(cuts))
        return jnp.repeat(jnp.exp(heights), extent[position] // blocks).reshape((-1,) + (1,) * (len(extent) - position - 1))

    factor_of = one(*cuts[0])
    for cut in cuts[1:]:
        factor_of = factor_of * one(*cut)
    return factor_of


def normal_values(own_key, dims, deviation, limit, cuts=(), kind=jnp.bfloat16):
    values = deviation * jax.random.normal(own_key, dims, jnp.float32)
    if cuts:
        values = values * shard_levels(own_key, dims, cuts, -0.22, 0.18)
    return jnp.clip(values, -limit, limit).astype(kind)


def setup_inputs(seed: int = 0) -> dict:
    streams_of = jax.random.split(jax.random.key(seed), 7)
    queries = draw_queries(jax.random.fold_in(streams_of[6], 71), 0)
    keys = draw_keys(jax.random.fold_in(streams_of[6], 71), 0)
    values = normal_values(streams_of[2], (TOKENS, HEADS * HD), 1.0, 6.0, ((0, 8), (1, 4)))
    out_weight = normal_values(streams_of[3], (D, HEADS * HD), (HEADS * HD) ** -0.5, 0.125, ((1, 4),))
    out_grad = normal_values(streams_of[4], (TOKENS, D), 1.0, 6.0, ((0, 8), (1, 4)))
    long_blocks = draw_long_blocks(jax.random.fold_in(streams_of[6], 71), 0)
    return {"queries": queries, "keys": keys, "values": values, "out_weight": out_weight, "out_grad": out_grad, "long_blocks": long_blocks}


highest = lax.Precision.HIGHEST

def split_heads(array):
    shaped = array.reshape(NBLK, BLOCK, N_HEAD, LIN_DEV + 1, HD)
    linear = shaped[:, :, :, :LIN_DEV].reshape(NBLK, BLOCK, N_HEAD * LIN_DEV, HD)
    sparse = shaped[:, :, :, LIN_DEV]
    return (linear, sparse)

def join_heads(linear, sparse):
    shaped = linear.reshape(NBLK, BLOCK, N_HEAD, LIN_DEV, HD)
    merged = jnp.concatenate([shaped, sparse[:, :, :, None]], axis=3)
    return merged.reshape(TOKENS, HEADS * HD)

def reference(queries, keys, values, out_weight, out_grad, long_blocks):
    causal = jnp.arange(BLOCK)[:, None] >= jnp.arange(BLOCK)[None, :]
    scaling = 1.0 / math.sqrt(HD)
    positions = jnp.arange(TOKENS, dtype=jnp.int32).reshape(NBLK, BLOCK)
    pos_scale = 1.0 / (math.sqrt(HD) * jnp.sqrt((positions + 1).astype(jnp.float32)))
    attn_grad = jnp.dot(out_grad, out_weight, preferred_element_type=jnp.float32).astype(jnp.bfloat16)
    lin_q, sparse_q = split_heads(queries)
    lin_k, sparse_k = split_heads(keys)
    lin_v, sparse_v = split_heads(values)
    lin_grad, sparse_grad = split_heads(attn_grad)

    def lin_scores_of(query_rows, key_rows, scale_row):
        scores = jnp.einsum('uhd,shd->hus', query_rows.astype(jnp.float32), key_rows.astype(jnp.float32))
        return jnp.where(causal[None], scale_row[None, :, None] * scores, 0.0).astype(jnp.bfloat16)

    def forward_step(state_now, block_in):
        query_rows, key_rows, value_rows, scale_row = block_in
        weights = lin_scores_of(query_rows, key_rows, scale_row)
        inside_block = jnp.einsum('hus,she->uhe', weights.astype(jnp.float32), value_rows.astype(jnp.float32))
        across = jnp.einsum('uhd,hde->uhe', query_rows.astype(jnp.float32), state_now, precision=highest)
        output = (inside_block + scale_row[:, None, None] * across).astype(jnp.bfloat16)
        state_next = state_now + jnp.einsum('shd,she->hde', key_rows.astype(jnp.float32), value_rows.astype(jnp.float32))
        return (state_next, (output, state_now))
    zero_state = jnp.zeros((N_HEAD * LIN_DEV, HD, HD), jnp.float32)
    final_state, (lin_out, state_before) = lax.scan(forward_step, zero_state, (lin_q, lin_k, lin_v, pos_scale))

    def backward_step(adj_after, block_in):
        query_rows, key_rows, value_rows, scale_row, grad_rows, state_now = block_in
        weights = lin_scores_of(query_rows, key_rows, scale_row)
        grad_scores = jnp.einsum('uhe,she->hus', grad_rows.astype(jnp.float32), value_rows.astype(jnp.float32))
        grad_weights = jnp.where(causal[None], scale_row[None, :, None] * grad_scores, 0.0).astype(jnp.bfloat16)
        scaled_grad = (scale_row[:, None, None] * grad_rows.astype(jnp.float32)).astype(jnp.bfloat16)
        grad_q = jnp.einsum('hus,shd->uhd', grad_weights.astype(jnp.float32), key_rows.astype(jnp.float32))
        grad_q = grad_q + scale_row[:, None, None] * jnp.einsum('uhe,hde->uhd', grad_rows.astype(jnp.float32), state_now, precision=highest)
        grad_k = jnp.einsum('hus,uhd->shd', grad_weights.astype(jnp.float32), query_rows.astype(jnp.float32))
        grad_k = grad_k + jnp.einsum('she,hde->shd', value_rows.astype(jnp.float32), adj_after, precision=highest)
        grad_v = jnp.einsum('hus,uhe->she', weights.astype(jnp.float32), grad_rows.astype(jnp.float32))
        grad_v = grad_v + jnp.einsum('shd,hde->she', key_rows.astype(jnp.float32), adj_after, precision=highest)
        adj_next = adj_after + jnp.einsum('uhd,uhe->hde', query_rows.astype(jnp.float32), scaled_grad.astype(jnp.float32))
        return (adj_next, (grad_q, grad_k, grad_v))
    total_adj, (lin_dq, lin_dk, lin_dv) = lax.scan(backward_step, zero_state, (lin_q, lin_k, lin_v, pos_scale, lin_grad, state_before), reverse=True)

    def sparse_step(block_in):
        query_rows, key_rows, value_rows, grad_rows, listed, index_here = block_in
        far_keys = jnp.take(sparse_k, listed, axis=0).astype(jnp.float32)
        far_values = jnp.take(sparse_v, listed, axis=0).astype(jnp.float32)
        usable = listed != index_here
        query_f = query_rows.astype(jnp.float32)
        key_f = key_rows.astype(jnp.float32)
        value_f = value_rows.astype(jnp.float32)
        grad_f = grad_rows.astype(jnp.float32)
        own_scores = scaling * jnp.einsum('uhd,shd->hus', query_f, key_f)
        own_scores = jnp.where(causal[None], own_scores, -jnp.inf)
        far_scores = scaling * jnp.einsum('uhd,rshd->hurs', query_f, far_keys)
        far_scores = jnp.where(usable[None, None, :, None], far_scores, -jnp.inf)
        row_peak = jnp.maximum(lax.optimization_barrier(jnp.max(own_scores, axis=2)), lax.optimization_barrier(jnp.max(far_scores, axis=(2, 3))))
        own_exp = jnp.exp(own_scores - row_peak[:, :, None])
        far_exp = jnp.exp(far_scores - row_peak[:, :, None, None])
        row_sums = lax.optimization_barrier(jnp.sum(own_exp, axis=2)) + lax.optimization_barrier(jnp.sum(far_exp, axis=(2, 3)))
        own_prob = own_exp / row_sums[:, :, None]
        far_prob = far_exp / row_sums[:, :, None, None]
        own_weight = own_prob.astype(jnp.bfloat16).astype(jnp.float32)
        far_weight = far_prob.astype(jnp.bfloat16).astype(jnp.float32)
        output = (jnp.einsum('hus,shd->uhd', own_weight, value_f) + jnp.einsum('hurs,rshd->uhd', far_weight, far_values)).astype(jnp.bfloat16)
        row_dot = lax.optimization_barrier(jnp.sum(grad_f * output.astype(jnp.float32), axis=-1)).T
        own_dp = jnp.einsum('uhd,shd->hus', grad_f, value_f)
        far_dp = jnp.einsum('uhd,rshd->hurs', grad_f, far_values)
        own_ds = (own_prob * (own_dp - row_dot[:, :, None])).astype(jnp.bfloat16).astype(jnp.float32)
        far_ds = (far_prob * (far_dp - row_dot[:, :, None, None])).astype(jnp.bfloat16).astype(jnp.float32)
        grad_q = scaling * (jnp.einsum('hus,shd->uhd', own_ds, key_f) + jnp.einsum('hurs,rshd->uhd', far_ds, far_keys))
        own_dk = scaling * jnp.einsum('hus,uhd->shd', own_ds, query_f)
        own_dv = jnp.einsum('hus,uhd->shd', own_weight, grad_f)
        pair_k = (scaling * jnp.einsum('hurs,uhd->rshd', far_ds, query_f)).astype(jnp.bfloat16)
        pair_v = jnp.einsum('hurs,uhd->rshd', far_weight, grad_f).astype(jnp.bfloat16)
        return (output, grad_q, own_dk, own_dv, pair_k, pair_v)
    block_ids = jnp.arange(NBLK, dtype=jnp.int32)
    sparse_out, sparse_dq, own_dk, own_dv, pair_k, pair_v = lax.map(sparse_step, (sparse_q, sparse_k, sparse_v, sparse_grad, long_blocks, block_ids))
    flat_ids = long_blocks.reshape(-1)
    far_dk = jax.ops.segment_sum(pair_k.reshape(NBLK * LISTED, BLOCK, N_HEAD, HD).astype(jnp.float32), flat_ids, num_segments=NBLK)
    far_dv = jax.ops.segment_sum(pair_v.reshape(NBLK * LISTED, BLOCK, N_HEAD, HD).astype(jnp.float32), flat_ids, num_segments=NBLK)
    sparse_dk = own_dk + far_dk
    sparse_dv = own_dv + far_dv
    attention = join_heads(lin_out, sparse_out)
    width = (LIN_DEV + 1) * HD
    layer_sum = jnp.zeros((TOKENS, D), jnp.float32)
    for group_id in range(N_HEAD):
        part_out = lax.dot_general(attention[:, group_id * width:(group_id + 1) * width], out_weight[:, group_id * width:(group_id + 1) * width], (((1,), (1,)), ((), ())), preferred_element_type=jnp.float32)
        rounded = lax.optimization_barrier(part_out.astype(jnp.bfloat16))
        layer_sum = layer_sum + rounded.astype(jnp.float32)
    layer_out = layer_sum.astype(jnp.bfloat16)
    query_grad = join_heads(lin_dq, sparse_dq).astype(jnp.bfloat16)
    key_grad = join_heads(lin_dk, sparse_dk).astype(jnp.bfloat16)
    value_grad = join_heads(lin_dv, sparse_dv).astype(jnp.bfloat16)
    return (layer_out, query_grad, key_grad, value_grad)
```

```python
import functools
import math

import jax
import jax.numpy as jnp
from jax import lax
from jax.experimental import pallas as pl
from jax.experimental.pallas import tpu as pltpu
from jax.sharding import PartitionSpec as P

HD = 128
LIN_DEV = 3
LISTED = 4
BLOCK = 512
CHUNK = 256
SCALING = 1.0 / math.sqrt(HD)
MESH = pl.DeviceIdType.MESH
VMEM_LIMIT = 56 * 1024 * 1024


def mm(a, b):
    return jnp.dot(a, b, preferred_element_type=jnp.float32)


def mm_nt(a, b):
    return lax.dot_general(a, b, (((1,), (1,)), ((), ())), preferred_element_type=jnp.float32)


def mm_tn(a, b):
    return lax.dot_general(a, b, (((0,), (0,)), ((), ())), preferred_element_type=jnp.float32)


def bf16(x):
    return x.astype(jnp.bfloat16)


def block_scale(ctx_place, row_count, b):
    first = ctx_place * row_count + b * BLOCK
    rows = lax.broadcasted_iota(jnp.int32, (BLOCK, HD), 0) + (first + 1)
    scale = 1.0 / (math.sqrt(HD) * jnp.sqrt(rows.astype(jnp.float32)))
    return scale


def causal_mask():
    u = lax.broadcasted_iota(jnp.int32, (BLOCK, BLOCK), 0)
    s = lax.broadcasted_iota(jnp.int32, (BLOCK, BLOCK), 1)
    return u >= s


def remote(src, dst, send, recv, target):
    return pltpu.make_async_remote_copy(
        src_ref=src, dst_ref=dst, send_sem=send, recv_sem=recv, device_id=target, device_id_type=MESH
    )


def enter(n_ctx, me, sib, par):
    barrier = pltpu.get_barrier_semaphore()
    for other in (sib, par):
        pl.semaphore_signal(barrier, inc=1, device_id={"head": other}, device_id_type=MESH)

    def greet(s, carry):
        to = lax.rem(me + s, n_ctx)
        pl.semaphore_signal(barrier, inc=1, device_id={"ctx": to}, device_id_type=MESH)
        return carry

    lax.fori_loop(1, n_ctx, greet, 0)
    pl.semaphore_wait(barrier, n_ctx + 1)


def gather_kernel(
    n_ctx, within, q, k, v, og, w,
    g_out, lin_out, state_out, kv_in,
    og_sib, og_par, og_far, kv_out, st_blk, st_out, st_in, total,
    sib_sems, par_send, par_recv, far_send, far_recv, kv_send, kv_recv, st_send, st_recv, own_sem,
):
    me = lax.axis_index("ctx")
    h = lax.axis_index("head")
    sib = h + 1 - 2 * lax.rem(h, 2)
    par = lax.rem(h + 2, 4)
    far = lax.rem(sib + 2, 4)
    rows, width = og.shape
    nblocks = rows // BLOCK
    chunks = rows // CHUNK
    enter(n_ctx, me, sib, par)

    def part(c):
        return pl.ds(pl.multiple_of(c * CHUNK, CHUNK), CHUNK)

    def par_copy(c):
        return remote(og.at[part(c)], og_par.at[part(c)], par_send.at[c], par_recv.at[c], {"head": par})

    def far_copy(c):
        return remote(og_par.at[part(c)], og_far.at[part(c)], far_send.at[c], far_recv.at[c], {"head": sib})

    sib_copy = remote(og, og_sib, sib_sems.at[0], sib_sems.at[1], {"head": sib})

    def kv_copy(s):
        to = lax.rem(me + s, n_ctx)
        return remote(kv_out.at[s], kv_in.at[me], kv_send.at[s], kv_recv.at[s], {"ctx": to})

    def st_copy(s):
        to = lax.rem(me + s, n_ctx)
        return remote(st_out, st_in.at[me], st_send.at[s], st_recv.at[s], {"ctx": to})

    def loop(first, last, step):
        def body(i, carry):
            step(i)
            return carry

        lax.fori_loop(first, last, body, 0)

    loop(0, chunks, lambda c: par_copy(c).start())

    def fill(s):
        to = lax.rem(me + s, n_ctx)
        picked_k = jnp.zeros((BLOCK, HD), jnp.float32)
        picked_v = jnp.zeros((BLOCK, HD), jnp.float32)
        for b in range(nblocks):
            here = slice(b * BLOCK, (b + 1) * BLOCK)
            chosen = within[to, b][:1]
            picked_k = picked_k + chosen * k[here, LIN_DEV * HD:].astype(jnp.float32)
            picked_v = picked_v + chosen * v[here, LIN_DEV * HD:].astype(jnp.float32)
        kv_out[s, :, :HD] = bf16(picked_k)
        kv_out[s, :, HD:] = bf16(picked_v)

    def fill_send(s):
        fill(s)
        kv_copy(s).start()

    loop(1, n_ctx, fill_send)
    sib_copy.start()
    fill(0)
    own_copy = pltpu.make_async_copy(kv_out.at[0], kv_in.at[me], own_sem)
    own_copy.start()

    for head in range(LIN_DEV):
        cols = slice(head * HD, (head + 1) * HD)
        device_state = jnp.zeros((HD, HD), jnp.float32)
        for b in range(nblocks):
            here = slice(b * BLOCK, (b + 1) * BLOCK)
            state = mm_tn(k[here, cols], v[here, cols])
            st_blk[b, head] = state
            device_state = device_state + state
        st_out[head] = bf16(device_state)
    loop(1, n_ctx, lambda s: st_copy(s).start())

    own_rows = pl.ds(pl.multiple_of(h * width, width), width)

    def own_product(c):
        total[part(c)] = mm(og[part(c)], w[own_rows])

    loop(0, chunks, own_product)
    loop(1, n_ctx, lambda s: st_copy(s).wait_recv())
    st_in[me] = st_out[...]
    for head in range(LIN_DEV):
        def earlier(j, state):
            return state + jnp.where(j < me, st_in[j, head].astype(jnp.float32), 0.0)

        state = lax.fori_loop(0, n_ctx, earlier, jnp.zeros((HD, HD), jnp.float32))
        for b in range(nblocks):
            state_out[b, head] = bf16(state)
            state = state + st_blk[b, head]

    for b in range(nblocks):
        scale = block_scale(me, rows, b)
        here = slice(b * BLOCK, (b + 1) * BLOCK)
        for head in range(LIN_DEV):
            cols = slice(head * HD, (head + 1) * HD)
            scores = mm_nt(q[here, cols], k[here, cols])
            weights = bf16(jnp.where(causal_mask(), scale[:, :1] * scores, 0.0))
            inside = mm(weights, v[here, cols])
            across = mm(q[here, cols], state_out[b, head])
            lin_out[here, cols] = bf16(inside + scale * across)

    par_rows = pl.ds(pl.multiple_of(par * width, width), width)
    sib_rows = pl.ds(pl.multiple_of(sib * width, width), width)
    far_rows = pl.ds(pl.multiple_of(far * width, width), width)

    sib_copy.wait_recv()

    def sib_product(c):
        total[part(c)] += mm(og_sib[part(c)], w[sib_rows])

    loop(0, chunks, sib_product)

    def forward(c):
        par_copy(c).wait_recv()
        far_copy(c).start()
        total[part(c)] += mm(og_par[part(c)], w[par_rows])

    loop(0, chunks, forward)

    def last(c):
        far_copy(c).wait_recv()
        g_out[part(c)] = bf16(total[part(c)] + mm(og_far[part(c)], w[far_rows]))

    loop(0, chunks, last)

    def finish(s):
        kv_copy(s).wait()
        st_copy(s).wait_send()

    loop(1, n_ctx, finish)

    def finish_chunk(c):
        par_copy(c).wait_send()
        far_copy(c).wait_send()

    loop(0, chunks, finish_chunk)
    sib_copy.wait_send()
    own_copy.wait()


def sparse_kernel(
    slots, usable, q, k, v, g, far0, far1, far2, far3,
    out, dq_out, dk_out, dv_out, pairs,
    probs, pair_buf, sems,
):
    b = pl.program_id(0)
    fars = (far0, far1, far2, far3)
    neg = jnp.float32(-jnp.inf)
    qb, kb, vb, gb = q[...], k[...], v[...], g[...]
    scores = jnp.where(causal_mask(), mm_nt(qb, kb), neg)
    probs[0] = scores
    peak = jnp.max(scores, axis=1, keepdims=True)
    for r in range(LISTED):
        bias = jnp.where(usable[b, r] != 0, jnp.float32(0.0), neg)
        scores = mm_nt(qb, fars[r][0, :, :HD]) + bias
        probs[r + 1] = scores
        peak = jnp.maximum(peak, jnp.max(scores, axis=1, keepdims=True))
    sums = jnp.zeros((BLOCK, 1), jnp.float32)
    for r in range(LISTED + 1):
        e = jnp.exp((probs[r] - peak) * SCALING)
        probs[r] = e
        sums = sums + jnp.sum(e, axis=1, keepdims=True)
    inv = 1.0 / sums
    result = jnp.zeros((BLOCK, HD), jnp.float32)
    for r in range(LISTED + 1):
        prob = probs[r] * inv
        probs[r] = prob
        weight = bf16(prob)
        val = vb if r == 0 else fars[r - 1][0, :, HD:]
        result = result + mm(weight, val)
        dv = mm_tn(weight, gb)
        if r == 0:
            dv_out[...] = dv
        else:
            pair_buf[r - 1, :, HD:] = bf16(dv)
    result = bf16(result)
    out[...] = result
    row_dot = jnp.sum(gb.astype(jnp.float32) * result.astype(jnp.float32), axis=1, keepdims=True)
    dq = jnp.zeros((BLOCK, HD), jnp.float32)
    for r in range(LISTED + 1):
        val = vb if r == 0 else fars[r - 1][0, :, HD:]
        key = kb if r == 0 else fars[r - 1][0, :, :HD]
        ds = bf16(probs[r] * (mm_nt(gb, val) - row_dot))
        dq = dq + mm(ds, key)
        dk = SCALING * mm_tn(ds, qb)
        if r == 0:
            dk_out[...] = dk
        else:
            pair_buf[r - 1, :, :HD] = bf16(dk)
    dq_out[...] = bf16(SCALING * dq)
    copies = [
        pltpu.make_async_copy(pair_buf.at[r], pairs.at[slots[b, r]], sems.at[r]) for r in range(LISTED)
    ]
    for copy in copies:
        copy.start()
    for copy in copies:
        copy.wait()


def scatter_kernel(
    n_ctx, back, q, k, v, g, w, lin, sp, state, dq_sp, dk_sp, dv_sp, pairs,
    layer, dq_out, dk_out, dv_out,
    ret, att, to_far, from_far, to_par, from_par, to_sib, from_sib, own, adj_blk, adj_out, adj_in, adj,
    ret_send, ret_recv, adj_send, adj_recv, far_send, far_recv, par_send, par_recv, sib_send, sib_recv, own_sem,
):
    me = lax.axis_index("ctx")
    h = lax.axis_index("head")
    sib = h + 1 - 2 * lax.rem(h, 2)
    par = lax.rem(h + 2, 4)
    far = lax.rem(sib + 2, 4)
    rows, width = own.shape
    nblocks = rows // BLOCK
    chunks = rows // CHUNK
    enter(n_ctx, me, sib, par)

    def part(c):
        return pl.ds(pl.multiple_of(c * CHUNK, CHUNK), CHUNK)

    def loop(first, last, step):
        def body(i, carry):
            step(i)
            return carry

        lax.fori_loop(first, last, body, 0)

    def ret_copy(s):
        to = lax.rem(me + s, n_ctx)
        return remote(pairs.at[to], ret.at[me], ret_send.at[s], ret_recv.at[s], {"ctx": to})

    def adj_copy(s):
        to = lax.rem(me + s, n_ctx)
        return remote(adj_out, adj_in.at[me], adj_send.at[s], adj_recv.at[s], {"ctx": to})

    def far_copy(c):
        return remote(to_far.at[part(c)], from_far.at[part(c)], far_send.at[c], far_recv.at[c], {"head": sib})

    def par_copy(c):
        return remote(to_par.at[part(c)], from_par.at[part(c)], par_send.at[c], par_recv.at[c], {"head": par})

    def sib_copy(c):
        return remote(to_sib.at[part(c)], from_sib.at[part(c)], sib_send.at[c], sib_recv.at[c], {"head": sib})

    loop(1, n_ctx, lambda s: ret_copy(s).start())
    own_copy = pltpu.make_async_copy(pairs.at[me], ret.at[me], own_sem)
    own_copy.start()
    att[:, :LIN_DEV * HD] = lin[...]
    att[:, LIN_DEV * HD:] = sp[...]

    def product(c, dest):
        return mm_nt(att[part(c)], w[pl.ds(pl.multiple_of(dest * width, width), width)])

    def far_step(c):
        to_far[part(c)] = bf16(product(c, far))
        far_copy(c).start()

    loop(0, chunks, far_step)

    def par_step(c):
        mine = product(c, par)
        far_copy(c).wait_recv()
        to_par[part(c)] = bf16(mine + from_far[part(c)].astype(jnp.float32))
        par_copy(c).start()

    loop(0, chunks, par_step)

    for head in range(LIN_DEV):
        cols = slice(head * HD, (head + 1) * HD)
        device_adj = jnp.zeros((HD, HD), jnp.float32)
        for b in range(nblocks):
            here = slice(b * BLOCK, (b + 1) * BLOCK)
            scaled = bf16(block_scale(me, rows, b) * g[here, cols].astype(jnp.float32))
            one = mm_tn(q[here, cols], scaled)
            adj_blk[b, head] = one
            device_adj = device_adj + one
        adj_out[head] = bf16(device_adj)
    loop(1, n_ctx, lambda s: adj_copy(s).start())

    def sib_step(c):
        to_sib[part(c)] = bf16(product(c, sib))
        sib_copy(c).start()

    loop(0, chunks, sib_step)

    def own_step(c):
        own[part(c)] = product(c, h)

    loop(0, chunks, own_step)

    loop(1, n_ctx, lambda s: adj_copy(s).wait_recv())
    adj_in[me] = adj_out[...]
    for head in range(LIN_DEV):
        def later(j, total):
            return total + jnp.where(j > me, adj_in[j, head].astype(jnp.float32), 0.0)

        total = lax.fori_loop(0, n_ctx, later, jnp.zeros((HD, HD), jnp.float32))
        for b in reversed(range(nblocks)):
            adj[b, head] = bf16(total)
            total = total + adj_blk[b, head]

    for b in range(nblocks):
        scale = block_scale(me, rows, b)
        here = slice(b * BLOCK, (b + 1) * BLOCK)
        for head in range(LIN_DEV):
            cols = slice(head * HD, (head + 1) * HD)
            qb, kb, vb, gb = q[here, cols], k[here, cols], v[here, cols], g[here, cols]
            keep = causal_mask()
            weights = bf16(jnp.where(keep, scale[:, :1] * mm_nt(qb, kb), 0.0))
            grads = bf16(jnp.where(keep, scale[:, :1] * mm_nt(gb, vb), 0.0))
            dq_out[here, cols] = bf16(mm(grads, kb) + scale * mm_nt(gb, state[b, head]))
            dk_out[here, cols] = bf16(mm_tn(grads, qb) + mm_nt(vb, adj[b, head]))
            dv_out[here, cols] = bf16(mm_tn(weights, gb) + mm(kb, adj[b, head]))
        dq_out[here, LIN_DEV * HD:] = dq_sp[here]

    own_copy.wait()
    loop(1, n_ctx, lambda s: ret_copy(s).wait())
    last = slice(LIN_DEV * HD, (LIN_DEV + 1) * HD)
    for b in range(nblocks):
        for t in range(BLOCK // HD):
            here = slice(t * HD, (t + 1) * HD)
            place = slice(b * BLOCK + t * HD, b * BLOCK + (t + 1) * HD)

            def add(j, sums):
                mine = back[j][:1] == b
                got = ret[j, here].astype(jnp.float32)
                return sums + jnp.where(mine, got, 0.0)

            sums = lax.fori_loop(0, n_ctx, add, jnp.zeros((HD, 2 * HD), jnp.float32))
            dk_out[place, last] = bf16(dk_sp[place] + sums[:, :HD])
            dv_out[place, last] = bf16(dv_sp[place] + sums[:, HD:])

    def final(c):
        sib_copy(c).wait()
        par_copy(c).wait()
        far_copy(c).wait_send()
        layer[part(c)] = bf16(
            own[part(c)] + from_sib[part(c)].astype(jnp.float32) + from_par[part(c)].astype(jnp.float32)
        )

    loop(0, chunks, final)
    loop(1, n_ctx, lambda s: adj_copy(s).wait_send())


def local(queries, keys, values, out_weight, out_grad, long_blocks):
    rows = queries.shape[0]
    nblocks = rows // BLOCK
    n_ctx = lax.axis_size("ctx")
    me = lax.axis_index("ctx")
    width = out_grad.shape[1]
    chunks = rows // CHUNK
    wide = LIN_DEV * HD
    requests = LISTED * nblocks
    table = long_blocks.reshape(n_ctx, requests)
    owners = table // nblocks
    inner = table % nblocks
    aimed = owners == me
    within = jnp.sum(jnp.where(aimed, inner, 0), axis=1).astype(jnp.int32)
    back = jnp.where(jnp.any(aimed, axis=1), within, -1).astype(jnp.int32)
    within = (within[:, None] == jnp.arange(nblocks)[None, :]).astype(jnp.float32)
    within = jnp.broadcast_to(within[:, :, None, None], (n_ctx, nblocks, 8, HD))
    back = jnp.broadcast_to(back[:, None, None], (n_ctx, 8, 2 * HD))
    lists = lax.dynamic_index_in_dim(table, me, 0, False).reshape(nblocks, LISTED)
    slots = (lists // nblocks).astype(jnp.int32)
    own_index = me * nblocks + jnp.arange(nblocks, dtype=jnp.int32)
    usable = (lists != own_index[:, None]).astype(jnp.int32)

    vmem = pl.BlockSpec(memory_space=pltpu.VMEM)
    anywhere = pl.BlockSpec(memory_space=pl.ANY)
    b16, f32 = jnp.bfloat16, jnp.float32
    dma = pltpu.SemaphoreType.DMA

    attn_grad, lin_out, state, kv_in = pl.pallas_call(
        functools.partial(gather_kernel, n_ctx),
        name="gather",
        out_shape=(
            jax.ShapeDtypeStruct((rows, wide + HD), b16),
            jax.ShapeDtypeStruct((rows, wide), b16),
            jax.ShapeDtypeStruct((nblocks, LIN_DEV, HD, HD), b16),
            jax.ShapeDtypeStruct((n_ctx, BLOCK, 2 * HD), b16),
        ),
        in_specs=[vmem] * 6,
        out_specs=(vmem, vmem, vmem, anywhere),
        scratch_shapes=[
            pltpu.VMEM((rows, width), b16),
            pltpu.VMEM((rows, width), b16),
            pltpu.VMEM((rows, width), b16),
            pltpu.VMEM((n_ctx, BLOCK, 2 * HD), b16),
            pltpu.VMEM((nblocks, LIN_DEV, HD, HD), f32),
            pltpu.VMEM((LIN_DEV, HD, HD), b16),
            pltpu.VMEM((n_ctx, LIN_DEV, HD, HD), b16),
            pltpu.VMEM((rows, wide + HD), f32),
            dma((2,)),
            dma((chunks,)),
            dma((chunks,)),
            dma((chunks,)),
            dma((chunks,)),
            dma((n_ctx,)),
            dma((n_ctx,)),
            dma((n_ctx,)),
            dma((n_ctx,)),
            dma(()),
        ],
        compiler_params=pltpu.CompilerParams(
            collective_id=0, has_side_effects=True, vmem_limit_bytes=VMEM_LIMIT
        ),
    )(within, queries, keys, values, out_grad, out_weight)

    column = pl.BlockSpec((BLOCK, HD), lambda b, slots, usable: (b, LIN_DEV))
    single = pl.BlockSpec((BLOCK, HD), lambda b, slots, usable: (b, 0))

    def far_spec(r):
        return pl.BlockSpec((1, BLOCK, 2 * HD), lambda b, slots, usable: (slots[b, r], 0, 0))

    sparse_out, dq_sp, dk_sp, dv_sp, pairs = pl.pallas_call(
        sparse_kernel,
        name="sparse",
        out_shape=(
            jax.ShapeDtypeStruct((rows, HD), b16),
            jax.ShapeDtypeStruct((rows, HD), b16),
            jax.ShapeDtypeStruct((rows, HD), f32),
            jax.ShapeDtypeStruct((rows, HD), f32),
            jax.ShapeDtypeStruct((n_ctx, BLOCK, 2 * HD), b16),
        ),
        grid_spec=pltpu.PrefetchScalarGridSpec(
            num_scalar_prefetch=2,
            grid=(nblocks,),
            in_specs=[column] * 4 + [far_spec(r) for r in range(LISTED)],
            out_specs=(single, single, single, single, anywhere),
            scratch_shapes=[
                pltpu.VMEM((LISTED + 1, BLOCK, BLOCK), f32),
                pltpu.VMEM((LISTED, BLOCK, 2 * HD), b16),
                dma((LISTED,)),
            ],
        ),
        compiler_params=pltpu.CompilerParams(vmem_limit_bytes=VMEM_LIMIT),
    )(slots, usable, queries, keys, values, attn_grad, kv_in, kv_in, kv_in, kv_in)

    big = pltpu.VMEM((rows, width), b16)
    return pl.pallas_call(
        functools.partial(scatter_kernel, n_ctx),
        name="scatter",
        out_shape=(
            jax.ShapeDtypeStruct((rows, width), b16),
            jax.ShapeDtypeStruct((rows, wide + HD), b16),
            jax.ShapeDtypeStruct((rows, wide + HD), b16),
            jax.ShapeDtypeStruct((rows, wide + HD), b16),
        ),
        in_specs=[vmem] * 12 + [anywhere],
        out_specs=(vmem, vmem, vmem, vmem),
        scratch_shapes=[
            pltpu.VMEM((n_ctx, BLOCK, 2 * HD), b16),
            pltpu.VMEM((rows, wide + HD), b16),
            big, big, big, big, big, big,
            pltpu.VMEM((rows, width), f32),
            pltpu.VMEM((nblocks, LIN_DEV, HD, HD), f32),
            pltpu.VMEM((LIN_DEV, HD, HD), b16),
            pltpu.VMEM((n_ctx, LIN_DEV, HD, HD), b16),
            pltpu.VMEM((nblocks, LIN_DEV, HD, HD), b16),
            dma((n_ctx,)),
            dma((n_ctx,)),
            dma((n_ctx,)),
            dma((n_ctx,)),
            dma((chunks,)),
            dma((chunks,)),
            dma((chunks,)),
            dma((chunks,)),
            dma((chunks,)),
            dma((chunks,)),
            dma(()),
        ],
        compiler_params=pltpu.CompilerParams(
            collective_id=1, has_side_effects=True, vmem_limit_bytes=VMEM_LIMIT
        ),
    )(
        back, queries, keys, values, attn_grad, out_weight, lin_out, sparse_out, state,
        dq_sp, dk_sp, dv_sp, pairs,
    )


def solution(mesh):
    return jax.shard_map(
        local,
        mesh=mesh,
        in_specs=(
            P("ctx", "head"),
            P("ctx", "head"),
            P("ctx", "head"),
            P(None, "head"),
            P("ctx", "head"),
            P(),
        ),
        out_specs=(P("ctx", "head"), P("ctx", "head"), P("ctx", "head"), P("ctx", "head")),
        check_vma=False,
    )
```

```python
import functools
import math

import jax
import jax.numpy as jnp
from jax import lax
from jax.experimental import pallas as pl
from jax.experimental.pallas import tpu as pltpu
from jax.sharding import PartitionSpec as P

HD = 128
LIN_DEV = 3
LISTED = 4
BLOCK = 512
CHUNK = 128
PAIR = 2
SCALING = 1.0 / math.sqrt(HD)
MESH = pl.DeviceIdType.MESH
VMEM_LIMIT = 56 * 1024 * 1024


def mm(a, b):
    return jnp.dot(a, b, preferred_element_type=jnp.float32)


def mm_nt(a, b):
    return lax.dot_general(a, b, (((1,), (1,)), ((), ())), preferred_element_type=jnp.float32)


def mm_tn(a, b):
    return lax.dot_general(a, b, (((0,), (0,)), ((), ())), preferred_element_type=jnp.float32)


def bf16(x):
    return x.astype(jnp.bfloat16)


def block_scale(ctx_place, row_count, b):
    first = ctx_place * row_count + b * BLOCK
    rows = lax.broadcasted_iota(jnp.int32, (BLOCK, HD), 0) + (first + 1)
    scale = 1.0 / (math.sqrt(HD) * jnp.sqrt(rows.astype(jnp.float32)))
    return scale


def causal_mask():
    u = lax.broadcasted_iota(jnp.int32, (BLOCK, BLOCK), 0)
    s = lax.broadcasted_iota(jnp.int32, (BLOCK, BLOCK), 1)
    return u >= s


def remote(src, dst, send, recv, target):
    return pltpu.make_async_remote_copy(
        src_ref=src, dst_ref=dst, send_sem=send, recv_sem=recv, device_id=target, device_id_type=MESH
    )


def enter(n_ctx, me, sib, par):
    barrier = pltpu.get_barrier_semaphore()
    for other in (sib, par):
        pl.semaphore_signal(barrier, inc=1, device_id={"head": other}, device_id_type=MESH)

    def greet(s, carry):
        to = lax.rem(me + s, n_ctx)
        pl.semaphore_signal(barrier, inc=1, device_id={"ctx": to}, device_id_type=MESH)
        return carry

    lax.fori_loop(1, n_ctx, greet, 0)
    pl.semaphore_wait(barrier, n_ctx + 1)


def gather_kernel(
    n_ctx, within, q, k, v, og, w,
    g_out, lin_out, state_out, kv_in,
    og_sib, og_par, og_far, kv_out, st_blk, st_out, st_in, total,
    sib_send, sib_recv, par_send, par_recv, far_send, far_recv, kv_send, kv_recv, st_send, st_recv, own_sem,
):
    me = lax.axis_index("ctx")
    h = lax.axis_index("head")
    sib = h + 1 - 2 * lax.rem(h, 2)
    par = lax.rem(h + 2, 4)
    far = lax.rem(sib + 2, 4)
    rows, width = og.shape
    nblocks = rows // BLOCK
    chunks = rows // CHUNK
    enter(n_ctx, me, sib, par)

    def part(c):
        return pl.ds(pl.multiple_of(c * CHUNK, CHUNK), CHUNK)

    def par_copy(c):
        return remote(og.at[part(c)], og_par.at[part(c)], par_send.at[c], par_recv.at[c], {"head": par})

    def far_copy(c):
        return remote(og_par.at[part(c)], og_far.at[part(c)], far_send.at[c], far_recv.at[c], {"head": sib})

    def sib_copy(c):
        return remote(og.at[part(c)], og_sib.at[part(c)], sib_send.at[c], sib_recv.at[c], {"head": sib})

    def kv_copy(s):
        to = lax.rem(me + s, n_ctx)
        return remote(kv_out.at[s], kv_in.at[me], kv_send.at[s], kv_recv.at[s], {"ctx": to})

    def st_copy(s):
        to = lax.rem(me + s, n_ctx)
        return remote(st_out, st_in.at[me], st_send.at[s], st_recv.at[s], {"ctx": to})

    def loop(first, last, step):
        def body(i, carry):
            step(i)
            return carry

        lax.fori_loop(first, last, body, 0)

    def fill(s):
        to = lax.rem(me + s, n_ctx)
        picked_k = jnp.zeros((BLOCK, HD), jnp.float32)
        picked_v = jnp.zeros((BLOCK, HD), jnp.float32)
        for b in range(nblocks):
            here = slice(b * BLOCK, (b + 1) * BLOCK)
            chosen = within[to, b][:1]
            picked_k = picked_k + chosen * k[here, LIN_DEV * HD:].astype(jnp.float32)
            picked_v = picked_v + chosen * v[here, LIN_DEV * HD:].astype(jnp.float32)
        kv_out[s, :, :HD] = bf16(picked_k)
        kv_out[s, :, HD:] = bf16(picked_v)

    def fill_send(s):
        fill(s)
        kv_copy(s).start()

    share = -(-(n_ctx - 1) // chunks)

    def start_step(c):
        par_copy(c).start()
        for i in range(share):
            s = 1 + c * share + i

            @pl.when(s < n_ctx)
            def _():
                fill_send(s)

        sib_copy(c).start()

    loop(0, chunks, start_step)
    fill(0)
    own_copy = pltpu.make_async_copy(kv_out.at[0], kv_in.at[me], own_sem)
    own_copy.start()

    for head in range(LIN_DEV):
        cols = slice(head * HD, (head + 1) * HD)
        device_state = jnp.zeros((HD, HD), jnp.float32)
        for b in range(nblocks):
            here = slice(b * BLOCK, (b + 1) * BLOCK)
            state = mm_tn(k[here, cols], v[here, cols])
            st_blk[b, head] = state
            device_state = device_state + state
        st_out[head] = bf16(device_state)
    loop(1, n_ctx, lambda s: st_copy(s).start())

    own_rows = pl.ds(pl.multiple_of(h * width, width), width)

    def pair(c):
        return pl.ds(pl.multiple_of(c * (PAIR * CHUNK), PAIR * CHUNK), PAIR * CHUNK)

    def own_product(c):
        total[pair(c)] = mm(og[pair(c)], w[own_rows])

    loop(0, chunks // PAIR, own_product)
    loop(1, n_ctx, lambda s: st_copy(s).wait_recv())
    st_in[me] = st_out[...]
    for head in range(LIN_DEV):
        def earlier(j, state):
            return state + jnp.where(j < me, st_in[j, head].astype(jnp.float32), 0.0)

        state = lax.fori_loop(0, n_ctx, earlier, jnp.zeros((HD, HD), jnp.float32))
        for b in range(nblocks):
            state_out[b, head] = bf16(state)
            state = state + st_blk[b, head]

    for b in range(nblocks):
        scale = block_scale(me, rows, b)
        here = slice(b * BLOCK, (b + 1) * BLOCK)
        for head in range(LIN_DEV):
            cols = slice(head * HD, (head + 1) * HD)
            scores = mm_nt(q[here, cols], k[here, cols])
            weights = bf16(jnp.where(causal_mask(), scale[:, :1] * scores, 0.0))
            inside = mm(weights, v[here, cols])
            across = mm(q[here, cols], state_out[b, head])
            lin_out[here, cols] = bf16(inside + scale * across)

    par_rows = pl.ds(pl.multiple_of(par * width, width), width)
    sib_rows = pl.ds(pl.multiple_of(sib * width, width), width)
    far_rows = pl.ds(pl.multiple_of(far * width, width), width)

    def sib_product(c):
        for i in range(PAIR):
            sib_copy(PAIR * c + i).wait_recv()
        total[pair(c)] += mm(og_sib[pair(c)], w[sib_rows])

    loop(0, chunks // PAIR, sib_product)

    def forward(c):
        for i in range(PAIR):
            par_copy(PAIR * c + i).wait_recv()
            far_copy(PAIR * c + i).start()
        total[pair(c)] += mm(og_par[pair(c)], w[par_rows])

    loop(0, chunks // PAIR, forward)

    def last(c):
        for i in range(PAIR):
            far_copy(PAIR * c + i).wait_recv()
        g_out[pair(c)] = bf16(total[pair(c)] + mm(og_far[pair(c)], w[far_rows]))

    loop(0, chunks // PAIR, last)

    def finish(s):
        kv_copy(s).wait()
        st_copy(s).wait_send()

    loop(1, n_ctx, finish)

    def finish_chunk(c):
        par_copy(c).wait_send()
        far_copy(c).wait_send()
        sib_copy(c).wait_send()

    loop(0, chunks, finish_chunk)
    own_copy.wait()


def sparse_kernel(
    slots, usable, q, k, v, g, far0, far1, far2, far3,
    out, dq_out, dk_out, dv_out, pairs,
    probs, pair_buf, sems,
):
    b = pl.program_id(0)
    fars = (far0, far1, far2, far3)
    neg = jnp.float32(-jnp.inf)
    qb, kb, vb, gb = q[...], k[...], v[...], g[...]
    scores = jnp.where(causal_mask(), mm_nt(qb, kb), neg)
    probs[0] = scores
    peak = jnp.max(scores, axis=1, keepdims=True)
    for r in range(LISTED):
        bias = jnp.where(usable[b, r] != 0, jnp.float32(0.0), neg)
        scores = mm_nt(qb, fars[r][0, :, :HD]) + bias
        probs[r + 1] = scores
        peak = jnp.maximum(peak, jnp.max(scores, axis=1, keepdims=True))
    sums = jnp.zeros((BLOCK, 1), jnp.float32)
    for r in range(LISTED + 1):
        e = jnp.exp((probs[r] - peak) * SCALING)
        probs[r] = e
        sums = sums + jnp.sum(e, axis=1, keepdims=True)
    inv = 1.0 / sums
    result = jnp.zeros((BLOCK, HD), jnp.float32)
    for r in range(LISTED + 1):
        prob = probs[r] * inv
        probs[r] = prob
        weight = bf16(prob)
        val = vb if r == 0 else fars[r - 1][0, :, HD:]
        result = result + mm(weight, val)
        dv = mm_tn(weight, gb)
        if r == 0:
            dv_out[...] = dv
        else:
            pair_buf[r - 1, :, HD:] = bf16(dv)
    result = bf16(result)
    out[...] = result
    row_dot = jnp.sum(gb.astype(jnp.float32) * result.astype(jnp.float32), axis=1, keepdims=True)
    dq = jnp.zeros((BLOCK, HD), jnp.float32)
    for r in range(LISTED + 1):
        val = vb if r == 0 else fars[r - 1][0, :, HD:]
        key = kb if r == 0 else fars[r - 1][0, :, :HD]
        ds = bf16(probs[r] * (mm_nt(gb, val) - row_dot))
        dq = dq + mm(ds, key)
        dk = SCALING * mm_tn(ds, qb)
        if r == 0:
            dk_out[...] = dk
        else:
            pair_buf[r - 1, :, :HD] = bf16(dk)
    dq_out[...] = bf16(SCALING * dq)
    copies = [
        pltpu.make_async_copy(pair_buf.at[r], pairs.at[slots[b, r]], sems.at[r]) for r in range(LISTED)
    ]
    for copy in copies:
        copy.start()
    for copy in copies:
        copy.wait()


def scatter_kernel(
    n_ctx, back, q, k, v, g, w, lin, sp, state, dq_sp, dk_sp, dv_sp, pairs,
    layer, dq_out, dk_out, dv_out,
    ret, att, to_far, from_far, to_par, from_par, to_sib, from_sib, own, adj_blk, adj_out, adj_in, adj,
    ret_send, ret_recv, adj_send, adj_recv, far_send, far_recv, par_send, par_recv, sib_send, sib_recv, own_sem,
):
    me = lax.axis_index("ctx")
    h = lax.axis_index("head")
    sib = h + 1 - 2 * lax.rem(h, 2)
    par = lax.rem(h + 2, 4)
    far = lax.rem(sib + 2, 4)
    rows, width = own.shape
    nblocks = rows // BLOCK
    chunks = rows // CHUNK
    enter(n_ctx, me, sib, par)

    def part(c):
        return pl.ds(pl.multiple_of(c * CHUNK, CHUNK), CHUNK)

    def loop(first, last, step):
        def body(i, carry):
            step(i)
            return carry

        lax.fori_loop(first, last, body, 0)

    def ret_copy(s):
        to = lax.rem(me + s, n_ctx)
        return remote(pairs.at[to], ret.at[me], ret_send.at[s], ret_recv.at[s], {"ctx": to})

    def adj_copy(s):
        to = lax.rem(me + s, n_ctx)
        return remote(adj_out, adj_in.at[me], adj_send.at[s], adj_recv.at[s], {"ctx": to})

    def far_copy(c):
        return remote(to_far.at[part(c)], from_far.at[part(c)], far_send.at[c], far_recv.at[c], {"head": sib})

    def par_copy(c):
        return remote(to_par.at[part(c)], from_par.at[part(c)], par_send.at[c], par_recv.at[c], {"head": par})

    def sib_copy(c):
        return remote(to_sib.at[part(c)], from_sib.at[part(c)], sib_send.at[c], sib_recv.at[c], {"head": sib})

    share = -(-(n_ctx - 1) // chunks)

    def ret_start(c):
        for i in range(share):
            s = 1 + c * share + i

            @pl.when(s < n_ctx)
            def _():
                ret_copy(s).start()

    ret_start(0)
    own_copy = pltpu.make_async_copy(pairs.at[me], ret.at[me], own_sem)
    own_copy.start()
    att[:, :LIN_DEV * HD] = lin[...]
    att[:, LIN_DEV * HD:] = sp[...]

    def pair(c):
        return pl.ds(pl.multiple_of(c * (PAIR * CHUNK), PAIR * CHUNK), PAIR * CHUNK)

    def product(c, dest):
        return mm_nt(att[pair(c)], w[pl.ds(pl.multiple_of(dest * width, width), width)])

    def far_step(c):
        to_far[pair(c)] = bf16(product(c, far))
        for i in range(PAIR):
            far_copy(PAIR * c + i).start()

    loop(0, chunks // PAIR, far_step)

    def par_step(c):
        mine = product(c, par)
        for i in range(PAIR):
            far_copy(PAIR * c + i).wait_recv()
        to_par[pair(c)] = bf16(mine + from_far[pair(c)].astype(jnp.float32))
        for i in range(PAIR):
            par_copy(PAIR * c + i).start()
            ret_start(PAIR * c + i + 1)

    loop(0, chunks // PAIR, par_step)

    for head in range(LIN_DEV):
        cols = slice(head * HD, (head + 1) * HD)
        device_adj = jnp.zeros((HD, HD), jnp.float32)
        for b in range(nblocks):
            here = slice(b * BLOCK, (b + 1) * BLOCK)
            scaled = bf16(block_scale(me, rows, b) * g[here, cols].astype(jnp.float32))
            one = mm_tn(q[here, cols], scaled)
            adj_blk[b, head] = one
            device_adj = device_adj + one
        adj_out[head] = bf16(device_adj)
    loop(1, n_ctx, lambda s: adj_copy(s).start())

    def sib_step(c):
        to_sib[pair(c)] = bf16(product(c, sib))
        for i in range(PAIR):
            sib_copy(PAIR * c + i).start()

    loop(0, chunks // PAIR, sib_step)

    def own_step(c):
        own[pair(c)] = product(c, h)

    loop(0, chunks // PAIR, own_step)

    loop(1, n_ctx, lambda s: adj_copy(s).wait_recv())
    adj_in[me] = adj_out[...]
    for head in range(LIN_DEV):
        def later(j, total):
            return total + jnp.where(j > me, adj_in[j, head].astype(jnp.float32), 0.0)

        total = lax.fori_loop(0, n_ctx, later, jnp.zeros((HD, HD), jnp.float32))
        for b in reversed(range(nblocks)):
            adj[b, head] = bf16(total)
            total = total + adj_blk[b, head]

    for b in range(nblocks):
        scale = block_scale(me, rows, b)
        here = slice(b * BLOCK, (b + 1) * BLOCK)
        for head in range(LIN_DEV):
            cols = slice(head * HD, (head + 1) * HD)
            qb, kb, vb, gb = q[here, cols], k[here, cols], v[here, cols], g[here, cols]
            keep = causal_mask()
            weights = bf16(jnp.where(keep, scale[:, :1] * mm_nt(qb, kb), 0.0))
            grads = bf16(jnp.where(keep, scale[:, :1] * mm_nt(gb, vb), 0.0))
            dq_out[here, cols] = bf16(mm(grads, kb) + scale * mm_nt(gb, state[b, head]))
            dk_out[here, cols] = bf16(mm_tn(grads, qb) + mm_nt(vb, adj[b, head]))
            dv_out[here, cols] = bf16(mm_tn(weights, gb) + mm(kb, adj[b, head]))
        dq_out[here, LIN_DEV * HD:] = dq_sp[here]

    own_copy.wait()
    loop(1, n_ctx, lambda s: ret_copy(s).wait())
    last = slice(LIN_DEV * HD, (LIN_DEV + 1) * HD)
    for b in range(nblocks):
        for t in range(BLOCK // HD):
            here = slice(t * HD, (t + 1) * HD)
            place = slice(b * BLOCK + t * HD, b * BLOCK + (t + 1) * HD)

            def add(j, sums):
                mine = back[j][:1] == b
                got = ret[j, here].astype(jnp.float32)
                return sums + jnp.where(mine, got, 0.0)

            sums = lax.fori_loop(0, n_ctx, add, jnp.zeros((HD, 2 * HD), jnp.float32))
            dk_out[place, last] = bf16(dk_sp[place] + sums[:, :HD])
            dv_out[place, last] = bf16(dv_sp[place] + sums[:, HD:])

    def final(c):
        sib_copy(c).wait()
        par_copy(c).wait()
        far_copy(c).wait_send()
        layer[part(c)] = bf16(
            own[part(c)] + from_sib[part(c)].astype(jnp.float32) + from_par[part(c)].astype(jnp.float32)
        )

    loop(0, chunks, final)
    loop(1, n_ctx, lambda s: adj_copy(s).wait_send())


def local(queries, keys, values, out_weight, out_grad, long_blocks):
    rows = queries.shape[0]
    nblocks = rows // BLOCK
    n_ctx = lax.axis_size("ctx")
    me = lax.axis_index("ctx")
    width = out_grad.shape[1]
    chunks = rows // CHUNK
    wide = LIN_DEV * HD
    requests = LISTED * nblocks
    table = long_blocks.reshape(n_ctx, requests)
    owners = table // nblocks
    inner = table % nblocks
    aimed = owners == me
    within = jnp.sum(jnp.where(aimed, inner, 0), axis=1).astype(jnp.int32)
    back = jnp.where(jnp.any(aimed, axis=1), within, -1).astype(jnp.int32)
    within = (within[:, None] == jnp.arange(nblocks)[None, :]).astype(jnp.float32)
    within = jnp.broadcast_to(within[:, :, None, None], (n_ctx, nblocks, 8, HD))
    back = jnp.broadcast_to(back[:, None, None], (n_ctx, 8, 2 * HD))
    lists = lax.dynamic_index_in_dim(table, me, 0, False).reshape(nblocks, LISTED)
    slots = (lists // nblocks).astype(jnp.int32)
    own_index = me * nblocks + jnp.arange(nblocks, dtype=jnp.int32)
    usable = (lists != own_index[:, None]).astype(jnp.int32)

    vmem = pl.BlockSpec(memory_space=pltpu.VMEM)
    anywhere = pl.BlockSpec(memory_space=pl.ANY)
    b16, f32 = jnp.bfloat16, jnp.float32
    dma = pltpu.SemaphoreType.DMA

    attn_grad, lin_out, state, kv_in = pl.pallas_call(
        functools.partial(gather_kernel, n_ctx),
        name="gather",
        out_shape=(
            jax.ShapeDtypeStruct((rows, wide + HD), b16),
            jax.ShapeDtypeStruct((rows, wide), b16),
            jax.ShapeDtypeStruct((nblocks, LIN_DEV, HD, HD), b16),
            jax.ShapeDtypeStruct((n_ctx, BLOCK, 2 * HD), b16),
        ),
        in_specs=[vmem] * 6,
        out_specs=(vmem, vmem, vmem, anywhere),
        scratch_shapes=[
            pltpu.VMEM((rows, width), b16),
            pltpu.VMEM((rows, width), b16),
            pltpu.VMEM((rows, width), b16),
            pltpu.VMEM((n_ctx, BLOCK, 2 * HD), b16),
            pltpu.VMEM((nblocks, LIN_DEV, HD, HD), f32),
            pltpu.VMEM((LIN_DEV, HD, HD), b16),
            pltpu.VMEM((n_ctx, LIN_DEV, HD, HD), b16),
            pltpu.VMEM((rows, wide + HD), f32),
            dma((chunks,)),
            dma((chunks,)),
            dma((chunks,)),
            dma((chunks,)),
            dma((chunks,)),
            dma((chunks,)),
            dma((n_ctx,)),
            dma((n_ctx,)),
            dma((n_ctx,)),
            dma((n_ctx,)),
            dma(()),
        ],
        compiler_params=pltpu.CompilerParams(
            collective_id=0, has_side_effects=True, vmem_limit_bytes=VMEM_LIMIT
        ),
    )(within, queries, keys, values, out_grad, out_weight)

    column = pl.BlockSpec((BLOCK, HD), lambda b, slots, usable: (b, LIN_DEV))
    single = pl.BlockSpec((BLOCK, HD), lambda b, slots, usable: (b, 0))

    def far_spec(r):
        return pl.BlockSpec((1, BLOCK, 2 * HD), lambda b, slots, usable: (slots[b, r], 0, 0))

    sparse_out, dq_sp, dk_sp, dv_sp, pairs = pl.pallas_call(
        sparse_kernel,
        name="sparse",
        out_shape=(
            jax.ShapeDtypeStruct((rows, HD), b16),
            jax.ShapeDtypeStruct((rows, HD), b16),
            jax.ShapeDtypeStruct((rows, HD), f32),
            jax.ShapeDtypeStruct((rows, HD), f32),
            jax.ShapeDtypeStruct((n_ctx, BLOCK, 2 * HD), b16),
        ),
        grid_spec=pltpu.PrefetchScalarGridSpec(
            num_scalar_prefetch=2,
            grid=(nblocks,),
            in_specs=[column] * 4 + [far_spec(r) for r in range(LISTED)],
            out_specs=(single, single, single, single, anywhere),
            scratch_shapes=[
                pltpu.VMEM((LISTED + 1, BLOCK, BLOCK), f32),
                pltpu.VMEM((LISTED, BLOCK, 2 * HD), b16),
                dma((LISTED,)),
            ],
        ),
        compiler_params=pltpu.CompilerParams(vmem_limit_bytes=VMEM_LIMIT),
    )(slots, usable, queries, keys, values, attn_grad, kv_in, kv_in, kv_in, kv_in)

    big = pltpu.VMEM((rows, width), b16)
    return pl.pallas_call(
        functools.partial(scatter_kernel, n_ctx),
        name="scatter",
        out_shape=(
            jax.ShapeDtypeStruct((rows, width), b16),
            jax.ShapeDtypeStruct((rows, wide + HD), b16),
            jax.ShapeDtypeStruct((rows, wide + HD), b16),
            jax.ShapeDtypeStruct((rows, wide + HD), b16),
        ),
        in_specs=[vmem] * 12 + [anywhere],
        out_specs=(vmem, vmem, vmem, vmem),
        scratch_shapes=[
            pltpu.VMEM((n_ctx, BLOCK, 2 * HD), b16),
            pltpu.VMEM((rows, wide + HD), b16),
            big, big, big, big, big, big,
            pltpu.VMEM((rows, width), f32),
            pltpu.VMEM((nblocks, LIN_DEV, HD, HD), f32),
            pltpu.VMEM((LIN_DEV, HD, HD), b16),
            pltpu.VMEM((n_ctx, LIN_DEV, HD, HD), b16),
            pltpu.VMEM((nblocks, LIN_DEV, HD, HD), b16),
            dma((n_ctx,)),
            dma((n_ctx,)),
            dma((n_ctx,)),
            dma((n_ctx,)),
            dma((chunks,)),
            dma((chunks,)),
            dma((chunks,)),
            dma((chunks,)),
            dma((chunks,)),
            dma((chunks,)),
            dma(()),
        ],
        compiler_params=pltpu.CompilerParams(
            collective_id=1, has_side_effects=True, vmem_limit_bytes=VMEM_LIMIT
        ),
    )(
        back, queries, keys, values, attn_grad, out_weight, lin_out, sparse_out, state,
        dq_sp, dk_sp, dv_sp, pairs,
    )


def solution(mesh):
    return jax.shard_map(
        local,
        mesh=mesh,
        in_specs=(
            P("ctx", "head"),
            P("ctx", "head"),
            P("ctx", "head"),
            P(None, "head"),
            P("ctx", "head"),
            P(),
        ),
        out_specs=(P("ctx", "head"), P("ctx", "head"), P("ctx", "head"), P("ctx", "head")),
        check_vma=False,
    )
```

```python
import functools
import math

import jax
import jax.numpy as jnp
from jax import lax
from jax.experimental import pallas as pl
from jax.experimental.pallas import tpu as pltpu
from jax.sharding import PartitionSpec as P

HD = 128
LIN_DEV = 3
LISTED = 4
BLOCK = 512
CHUNK = 128
PAIR = 2
SCALING = 1.0 / math.sqrt(HD)
MESH = pl.DeviceIdType.MESH
VMEM_LIMIT = 56 * 1024 * 1024


def mm(a, b):
    return jnp.dot(a, b, preferred_element_type=jnp.float32)


def mm_nt(a, b):
    return lax.dot_general(a, b, (((1,), (1,)), ((), ())), preferred_element_type=jnp.float32)


def mm_tn(a, b):
    return lax.dot_general(a, b, (((0,), (0,)), ((), ())), preferred_element_type=jnp.float32)


def bf16(x):
    return x.astype(jnp.bfloat16)


def block_scale(ctx_place, row_count, b):
    first = ctx_place * row_count + b * BLOCK
    rows = lax.broadcasted_iota(jnp.int32, (BLOCK, HD), 0) + (first + 1)
    scale = 1.0 / (math.sqrt(HD) * jnp.sqrt(rows.astype(jnp.float32)))
    return scale


def causal_mask():
    u = lax.broadcasted_iota(jnp.int32, (BLOCK, BLOCK), 0)
    s = lax.broadcasted_iota(jnp.int32, (BLOCK, BLOCK), 1)
    return u >= s


def remote(src, dst, send, recv, target):
    return pltpu.make_async_remote_copy(
        src_ref=src, dst_ref=dst, send_sem=send, recv_sem=recv, device_id=target, device_id_type=MESH
    )


def enter(n_ctx, me, sib, par):
    barrier = pltpu.get_barrier_semaphore()
    for other in (sib, par):
        pl.semaphore_signal(barrier, inc=1, device_id={"head": other}, device_id_type=MESH)

    def greet(s, carry):
        to = lax.rem(me + s, n_ctx)
        pl.semaphore_signal(barrier, inc=1, device_id={"ctx": to}, device_id_type=MESH)
        return carry

    lax.fori_loop(1, n_ctx, greet, 0)
    pl.semaphore_wait(barrier, n_ctx + 1)


def loop(first, last, step):
    def body(i, carry):
        step(i)
        return carry

    lax.fori_loop(first, last, body, 0)


def asked(table, place, block, nblocks):
    count = jnp.int32(0)
    for i in range(nblocks):
        for r in range(LISTED):
            count = count + (table[place * nblocks + i, r] == block).astype(jnp.int32)
    return count


def gather_kernel(
    n_ctx, table, q, k, v, og, w,
    own_out, partial_out, lin_out, state_out, kv_in, w_out,
    og_both, w_par, kv_out, st_blk, st_out, st_in, total,
    sib_send, sib_recv, w_send, w_recv, kv_send, kv_recv, st_send, st_recv, own_sem, w_sem,
):
    me = lax.axis_index("ctx")
    h = lax.axis_index("head")
    side = lax.rem(h, 2)
    sib = h + 1 - 2 * side
    par = lax.rem(h + 2, 4)
    rows, width = og.shape
    nblocks = rows // BLOCK
    chunks = rows // CHUNK
    tall = 2 * width // chunks
    enter(n_ctx, me, sib, par)

    def part(c):
        return pl.ds(pl.multiple_of(c * CHUNK, CHUNK), CHUNK)

    def sib_copy(c):
        return remote(
            og.at[part(c)], og_both.at[side, part(c)], sib_send.at[c], sib_recv.at[c], {"head": sib}
        )

    def w_copy(c):
        first = (par - side) * width + c * tall
        source = pl.ds(pl.multiple_of(first, tall), tall)
        target = pl.ds(pl.multiple_of(c * tall, tall), tall)
        return remote(w.at[source], w_par.at[target], w_send.at[c], w_recv.at[c], {"head": par})

    def kv_copy(s):
        to = lax.rem(me + s, n_ctx)
        return remote(kv_out.at[s], kv_in.at[me], kv_send.at[s], kv_recv.at[s], {"ctx": to})

    def st_copy(s):
        to = lax.rem(me + s, n_ctx)
        return remote(st_out, st_in.at[me], st_send.at[s], st_recv.at[s], {"ctx": to})

    def fill(s):
        to = lax.rem(me + s, n_ctx)
        picked_k = jnp.zeros((BLOCK, HD), jnp.float32)
        picked_v = jnp.zeros((BLOCK, HD), jnp.float32)
        for b in range(nblocks):
            here = slice(b * BLOCK, (b + 1) * BLOCK)
            chosen = asked(table, to, me * nblocks + b, nblocks).astype(jnp.float32)
            picked_k = picked_k + chosen * k[here, LIN_DEV * HD:].astype(jnp.float32)
            picked_v = picked_v + chosen * v[here, LIN_DEV * HD:].astype(jnp.float32)
        kv_out[s, :, :HD] = bf16(picked_k)
        kv_out[s, :, HD:] = bf16(picked_v)

    share = -(-(n_ctx - 1) // chunks)

    def start_step(c):
        w_copy(c).start()
        sib_copy(c).start()
        for i in range(share):
            s = 1 + c * share + i

            @pl.when(s < n_ctx)
            def _():
                fill(s)
                kv_copy(s).start()

    loop(0, chunks, start_step)
    fill(0)
    own_copy = pltpu.make_async_copy(kv_out.at[0], kv_in.at[me], own_sem)
    own_copy.start()

    for head in range(LIN_DEV):
        cols = slice(head * HD, (head + 1) * HD)
        device_state = jnp.zeros((HD, HD), jnp.float32)
        for b in range(nblocks):
            here = slice(b * BLOCK, (b + 1) * BLOCK)
            state = mm_tn(k[here, cols], v[here, cols])
            st_blk[b, head] = state
            device_state = device_state + state
        st_out[head] = bf16(device_state)
    loop(1, n_ctx, lambda s: st_copy(s).start())

    def pair(c):
        return pl.ds(pl.multiple_of(c * (PAIR * CHUNK), PAIR * CHUNK), PAIR * CHUNK)

    own_rows = pl.ds(pl.multiple_of(h * width, width), width)
    sib_rows = pl.ds(pl.multiple_of(sib * width, width), width)

    def own_product(c):
        og_both[side, pair(c)] = og[pair(c)]
        own_out[pair(c)] = mm(og[pair(c)], w[own_rows])

    loop(0, chunks // PAIR, own_product)
    loop(1, n_ctx, lambda s: st_copy(s).wait_recv())
    st_in[me] = st_out[...]
    for head in range(LIN_DEV):
        def earlier(j, state):
            return state + jnp.where(j < me, st_in[j, head].astype(jnp.float32), 0.0)

        state = lax.fori_loop(0, n_ctx, earlier, jnp.zeros((HD, HD), jnp.float32))
        for b in range(nblocks):
            state_out[b, head] = bf16(state)
            state = state + st_blk[b, head]

    for b in range(nblocks):
        scale = block_scale(me, rows, b)
        here = slice(b * BLOCK, (b + 1) * BLOCK)
        for head in range(LIN_DEV):
            cols = slice(head * HD, (head + 1) * HD)
            scores = mm_nt(q[here, cols], k[here, cols])
            weights = bf16(jnp.where(causal_mask(), scale[:, :1] * scores, 0.0))
            inside = mm(weights, v[here, cols])
            across = mm(q[here, cols], state_out[b, head])
            lin_out[here, cols] = bf16(inside + scale * across)

    def sib_product(c):
        for i in range(PAIR):
            sib_copy(PAIR * c + i).wait_recv()
        own_out[pair(c)] += mm(og_both[1 - side, pair(c)], w[sib_rows])

    loop(0, chunks // PAIR, sib_product)

    pieces = 4
    deep = 2 * width // pieces
    for piece in range(pieces):
        for i in range(chunks // pieces):
            w_copy(piece * (chunks // pieces) + i).wait_recv()
        half = piece * deep // width
        cols = slice(piece * deep - half * width, (piece + 1) * deep - half * width)
        inner = slice(piece * deep, (piece + 1) * deep)

        def par_product(c):
            value = mm(og_both[half, pair(c), cols], w_par[inner])
            if piece > 0:
                value = value + total[pair(c)]
            if piece < pieces - 1:
                total[pair(c)] = value
            else:
                partial_out[pair(c)] = bf16(value)

        loop(0, chunks // PAIR, par_product)
    w_copy_out = pltpu.make_async_copy(w_par, w_out, w_sem)
    w_copy_out.start()

    def finish(s):
        kv_copy(s).wait()
        st_copy(s).wait_send()

    loop(1, n_ctx, finish)

    def finish_chunk(c):
        w_copy(c).wait_send()
        sib_copy(c).wait_send()

    loop(0, chunks, finish_chunk)
    own_copy.wait()
    w_copy_out.wait()


def forward_kernel(table, place, q, k, v, far0, far1, far2, far3, out, weights, probs):
    b = pl.program_id(0)
    here = place[0] * pl.num_programs(0) + b
    fars = (far0, far1, far2, far3)
    neg = jnp.float32(-jnp.inf)
    qb, kb, vb = q[...], k[...], v[...]
    scores = jnp.where(causal_mask(), mm_nt(qb, kb), neg)
    probs[0] = scores
    peak = jnp.max(scores, axis=1, keepdims=True)
    for r in range(LISTED):
        bias = jnp.where(table[here, r] != here, jnp.float32(0.0), neg)
        scores = mm_nt(qb, fars[r][0, :, :HD]) + bias
        probs[r + 1] = scores
        peak = jnp.maximum(peak, jnp.max(scores, axis=1, keepdims=True))
    sums = jnp.zeros((BLOCK, 1), jnp.float32)
    for r in range(LISTED + 1):
        e = jnp.exp((probs[r] - peak) * SCALING)
        probs[r] = e
        sums = sums + jnp.sum(e, axis=1, keepdims=True)
    inv = 1.0 / sums
    result = jnp.zeros((BLOCK, HD), jnp.float32)
    for r in range(LISTED + 1):
        weight = bf16(probs[r] * inv)
        weights[0, r] = weight
        result = result + mm(weight, vb if r == 0 else fars[r - 1][0, :, HD:])
    out[...] = bf16(result)


def backward_kernel(
    table, place, q, k, v, own, other, out, weights, far0, far1, far2, far3,
    dq_out, dk_out, dv_out, pairs, pair_buf, sems,
):
    b = pl.program_id(0)
    nblocks = pl.num_programs(0)
    here = place[0] * nblocks + b
    fars = (far0, far1, far2, far3)
    qb, kb, vb = q[...], k[...], v[...]
    gb = bf16(own[...] + other[...].astype(jnp.float32))
    row_dot = jnp.sum(gb.astype(jnp.float32) * out[...].astype(jnp.float32), axis=1, keepdims=True)
    copies = [
        pltpu.make_async_copy(pair_buf.at[r], pairs.at[table[here, r] // nblocks], sems.at[r])
        for r in range(LISTED)
    ]
    dq = jnp.zeros((BLOCK, HD), jnp.float32)
    for r in (1, 2, 3, 4, 0):
        weight = weights[0, r]
        val = vb if r == 0 else fars[r - 1][0, :, HD:]
        key = kb if r == 0 else fars[r - 1][0, :, :HD]
        ds = bf16(weight.astype(jnp.float32) * (mm_nt(gb, val) - row_dot))
        dv = mm_tn(weight, gb)
        dq = dq + mm(ds, key)
        dk = SCALING * mm_tn(ds, qb)
        if r == 0:
            dk_out[...] = dk
            dv_out[...] = dv
        else:
            pair_buf[r - 1, :, :HD] = bf16(dk)
            pair_buf[r - 1, :, HD:] = bf16(dv)
            copies[r - 1].start()
    dq_out[...] = bf16(SCALING * dq)
    for copy in copies:
        copy.wait()


def scatter_kernel(
    n_ctx, table, q, k, v, own, other, w, w_par, lin, sp, state, dq_sp, dk_sp, dv_sp, pairs,
    layer, dq_out, dk_out, dv_out,
    ret, att, att_par, g, to_sib, from_sib, total, adj_blk, adj_out, adj_in, adj,
    ret_send, ret_recv, adj_send, adj_recv, att_send, att_recv, sib_send, sib_recv, own_sem,
):
    me = lax.axis_index("ctx")
    h = lax.axis_index("head")
    side = lax.rem(h, 2)
    sib = h + 1 - 2 * side
    par = lax.rem(h + 2, 4)
    rows, width = total.shape
    nblocks = rows // BLOCK
    steps = rows // (PAIR * CHUNK)
    enter(n_ctx, me, sib, par)

    def pair(c):
        return pl.ds(pl.multiple_of(c * (PAIR * CHUNK), PAIR * CHUNK), PAIR * CHUNK)

    def ret_copy(s):
        to = lax.rem(me + s, n_ctx)
        return remote(pairs.at[to], ret.at[me], ret_send.at[s], ret_recv.at[s], {"ctx": to})

    def adj_copy(s):
        to = lax.rem(me + s, n_ctx)
        return remote(adj_out, adj_in.at[me], adj_send.at[s], adj_recv.at[s], {"ctx": to})

    def att_copy(c):
        return remote(att.at[pair(c)], att_par.at[pair(c)], att_send.at[c], att_recv.at[c], {"head": par})

    def sib_copy(c):
        return remote(to_sib.at[pair(c)], from_sib.at[pair(c)], sib_send.at[c], sib_recv.at[c], {"head": sib})

    att[:, :LIN_DEV * HD] = lin[...]
    att[:, LIN_DEV * HD:] = sp[...]
    share = -(-(n_ctx - 1) // steps)

    def start_step(c):
        att_copy(c).start()
        for i in range(share):
            s = 1 + c * share + i

            @pl.when(s < n_ctx)
            def _():
                ret_copy(s).start()

    loop(0, steps, start_step)
    own_copy = pltpu.make_async_copy(pairs.at[me], ret.at[me], own_sem)
    own_copy.start()

    for head in range(LIN_DEV):
        cols = slice(head * HD, (head + 1) * HD)
        device_adj = jnp.zeros((HD, HD), jnp.float32)
        for b in range(nblocks):
            here = slice(b * BLOCK, (b + 1) * BLOCK)
            gb = bf16(own[here, cols] + other[here, cols].astype(jnp.float32))
            g[here, cols] = gb
            scaled = bf16(block_scale(me, rows, b) * gb.astype(jnp.float32))
            one = mm_tn(q[here, cols], scaled)
            adj_blk[b, head] = one
            device_adj = device_adj + one
        adj_out[head] = bf16(device_adj)
    loop(1, n_ctx, lambda s: adj_copy(s).start())

    def rows_of(which):
        return pl.ds(pl.multiple_of(which * width, width), width)

    def sib_step(c):
        mine = mm_nt(att[pair(c)], w[rows_of(sib)])
        total[pair(c)] = mm_nt(att[pair(c)], w[rows_of(h)])
        att_copy(c).wait_recv()
        to_sib[pair(c)] = bf16(mine + mm_nt(att_par[pair(c)], w_par[rows_of(1 - side)]))
        sib_copy(c).start()
        total[pair(c)] += mm_nt(att_par[pair(c)], w_par[rows_of(side)])

    loop(0, steps, sib_step)

    loop(1, n_ctx, lambda s: adj_copy(s).wait_recv())
    adj_in[me] = adj_out[...]
    for head in range(LIN_DEV):
        def later(j, value):
            return value + jnp.where(j > me, adj_in[j, head].astype(jnp.float32), 0.0)

        value = lax.fori_loop(0, n_ctx, later, jnp.zeros((HD, HD), jnp.float32))
        for b in reversed(range(nblocks)):
            adj[b, head] = bf16(value)
            value = value + adj_blk[b, head]

    for b in range(nblocks):
        scale = block_scale(me, rows, b)
        here = slice(b * BLOCK, (b + 1) * BLOCK)
        for head in range(LIN_DEV):
            cols = slice(head * HD, (head + 1) * HD)
            qb, kb, vb, gb = q[here, cols], k[here, cols], v[here, cols], g[here, cols]
            keep = causal_mask()
            weights = bf16(jnp.where(keep, scale[:, :1] * mm_nt(qb, kb), 0.0))
            grads = bf16(jnp.where(keep, scale[:, :1] * mm_nt(gb, vb), 0.0))
            dq_out[here, cols] = bf16(mm(grads, kb) + scale * mm_nt(gb, state[b, head]))
            dk_out[here, cols] = bf16(mm_tn(grads, qb) + mm_nt(vb, adj[b, head]))
            dv_out[here, cols] = bf16(mm_tn(weights, gb) + mm(kb, adj[b, head]))
        dq_out[here, LIN_DEV * HD:] = dq_sp[here]

    def final(c):
        sib_copy(c).wait()
        att_copy(c).wait_send()
        layer[pair(c)] = bf16(total[pair(c)] + from_sib[pair(c)].astype(jnp.float32))

    loop(0, steps, final)

    own_copy.wait()
    loop(1, n_ctx, lambda s: ret_copy(s).wait())
    last = slice(LIN_DEV * HD, (LIN_DEV + 1) * HD)
    for b in range(nblocks):
        for t in range(BLOCK // HD):
            here = slice(t * HD, (t + 1) * HD)
            place = slice(b * BLOCK + t * HD, b * BLOCK + (t + 1) * HD)

            def add(j, sums):
                count = asked(table, j, me * nblocks + b, nblocks)
                mine = jnp.full((1, 2 * HD), count, jnp.int32) > 0
                got = ret[j, here].astype(jnp.float32)
                return sums + jnp.where(mine, got, 0.0)

            sums = lax.fori_loop(0, n_ctx, add, jnp.zeros((HD, 2 * HD), jnp.float32))
            dk_out[place, last] = bf16(dk_sp[place] + sums[:, :HD])
            dv_out[place, last] = bf16(dv_sp[place] + sums[:, HD:])
    loop(1, n_ctx, lambda s: adj_copy(s).wait_send())


def local(queries, keys, values, out_weight, out_grad, long_blocks):
    rows = queries.shape[0]
    nblocks = rows // BLOCK
    n_ctx = lax.axis_size("ctx")
    place = lax.axis_index("ctx").astype(jnp.int32).reshape(1)
    width = out_grad.shape[1]
    chunks = rows // CHUNK
    steps = chunks // PAIR
    wide = LIN_DEV * HD
    full = wide + HD

    vmem = pl.BlockSpec(memory_space=pltpu.VMEM)
    smem = pl.BlockSpec(memory_space=pltpu.SMEM)
    anywhere = pl.BlockSpec(memory_space=pl.ANY)
    b16, f32 = jnp.bfloat16, jnp.float32
    shape = jax.ShapeDtypeStruct

    def sems(*counts):
        return [pltpu.SemaphoreType.DMA((n,)) for n in counts]

    single_sem = pltpu.SemaphoreType.DMA(())

    own, partial, lin_out, state, kv_in, w_par = pl.pallas_call(
        functools.partial(gather_kernel, n_ctx),
        name="gather",
        out_shape=(
            shape((rows, full), f32),
            shape((rows, full), b16),
            shape((rows, wide), b16),
            shape((nblocks, LIN_DEV, HD, HD), b16),
            shape((n_ctx, BLOCK, 2 * HD), b16),
            shape((2 * width, full), b16),
        ),
        in_specs=[smem] + [vmem] * 5,
        out_specs=(vmem, vmem, vmem, vmem, anywhere, anywhere),
        scratch_shapes=[
            pltpu.VMEM((2, rows, width), b16),
            pltpu.VMEM((2 * width, full), b16),
            pltpu.VMEM((n_ctx, BLOCK, 2 * HD), b16),
            pltpu.VMEM((nblocks, LIN_DEV, HD, HD), f32),
            pltpu.VMEM((LIN_DEV, HD, HD), b16),
            pltpu.VMEM((n_ctx, LIN_DEV, HD, HD), b16),
            pltpu.VMEM((rows, full), f32),
            *sems(chunks, chunks, chunks, chunks, n_ctx, n_ctx, n_ctx, n_ctx),
            single_sem,
            single_sem,
        ],
        compiler_params=pltpu.CompilerParams(
            collective_id=0, has_side_effects=True, vmem_limit_bytes=VMEM_LIMIT
        ),
    )(long_blocks, queries, keys, values, out_grad, out_weight)

    heads = lax.axis_size("head")
    other = lax.ppermute(partial, "head", [(i, (i + 2) % heads) for i in range(heads)])

    column = pl.BlockSpec((BLOCK, HD), lambda b, table, place: (b, LIN_DEV))
    single = pl.BlockSpec((BLOCK, HD), lambda b, table, place: (b, 0))
    squares = pl.BlockSpec((1, LISTED + 1, BLOCK, BLOCK), lambda b, table, place: (b, 0, 0, 0))

    def far_spec(r):
        return pl.BlockSpec(
            (1, BLOCK, 2 * HD),
            lambda b, table, place: (table[place[0] * nblocks + b, r] // nblocks, 0, 0),
        )

    fars = [far_spec(r) for r in range(LISTED)]
    flops = 2 * 2 * rows * (LISTED + 1) * BLOCK * HD
    sparse_out, weights = pl.pallas_call(
        forward_kernel,
        name="sparse_forward",
        out_shape=(shape((rows, HD), b16), shape((nblocks, LISTED + 1, BLOCK, BLOCK), b16)),
        grid_spec=pltpu.PrefetchScalarGridSpec(
            num_scalar_prefetch=2,
            grid=(nblocks,),
            in_specs=[column] * 3 + fars,
            out_specs=(single, squares),
            scratch_shapes=[pltpu.VMEM((LISTED + 1, BLOCK, BLOCK), f32)],
        ),
        compiler_params=pltpu.CompilerParams(vmem_limit_bytes=VMEM_LIMIT),
        cost_estimate=pl.CostEstimate(flops=3 * flops, bytes_accessed=20 * 2**20, transcendentals=0),
    )(long_blocks, place, queries, keys, values, kv_in, kv_in, kv_in, kv_in)

    dq_sp, dk_sp, dv_sp, pairs = pl.pallas_call(
        backward_kernel,
        name="sparse_backward",
        out_shape=(
            shape((rows, HD), b16),
            shape((rows, HD), f32),
            shape((rows, HD), f32),
            shape((n_ctx, BLOCK, 2 * HD), b16),
        ),
        grid_spec=pltpu.PrefetchScalarGridSpec(
            num_scalar_prefetch=2,
            grid=(nblocks,),
            in_specs=[column] * 5 + [single, squares] + fars,
            out_specs=(single, single, single, anywhere),
            scratch_shapes=[pltpu.VMEM((LISTED, BLOCK, 2 * HD), b16), *sems(LISTED)],
        ),
        compiler_params=pltpu.CompilerParams(vmem_limit_bytes=VMEM_LIMIT),
    )(long_blocks, place, queries, keys, values, own, other, sparse_out, weights, kv_in, kv_in, kv_in, kv_in)

    big = pltpu.VMEM((rows, width), b16)
    tokens = pltpu.VMEM((rows, full), b16)
    return pl.pallas_call(
        functools.partial(scatter_kernel, n_ctx),
        name="scatter",
        out_shape=(
            shape((rows, width), b16),
            shape((rows, full), b16),
            shape((rows, full), b16),
            shape((rows, full), b16),
        ),
        in_specs=[smem] + [vmem] * 13 + [anywhere],
        out_specs=(vmem, vmem, vmem, vmem),
        scratch_shapes=[
            pltpu.VMEM((n_ctx, BLOCK, 2 * HD), b16),
            tokens, tokens, tokens,
            big, big,
            pltpu.VMEM((rows, width), f32),
            pltpu.VMEM((nblocks, LIN_DEV, HD, HD), f32),
            pltpu.VMEM((LIN_DEV, HD, HD), b16),
            pltpu.VMEM((n_ctx, LIN_DEV, HD, HD), b16),
            pltpu.VMEM((nblocks, LIN_DEV, HD, HD), b16),
            *sems(n_ctx, n_ctx, n_ctx, n_ctx, steps, steps, steps, steps),
            single_sem,
        ],
        compiler_params=pltpu.CompilerParams(
            collective_id=1, has_side_effects=True, vmem_limit_bytes=VMEM_LIMIT
        ),
    )(
        long_blocks, queries, keys, values, own, other, out_weight, w_par, lin_out, sparse_out, state,
        dq_sp, dk_sp, dv_sp, pairs,
    )


def solution(mesh):
    return jax.shard_map(
        local,
        mesh=mesh,
        in_specs=(
            P("ctx", "head"),
            P("ctx", "head"),
            P("ctx", "head"),
            P(None, "head"),
            P("ctx", "head"),
            P(),
        ),
        out_specs=(P("ctx", "head"), P("ctx", "head"), P("ctx", "head"), P("ctx", "head")),
        check_vma=False,
    )
```

```python
import functools
import math

import jax
import jax.numpy as jnp
from jax import lax
from jax.experimental import pallas as pl
from jax.experimental.pallas import tpu as pltpu
from jax.sharding import PartitionSpec as P

HD = 128
LIN_DEV = 3
LISTED = 4
BLOCK = 512
CHUNK = 256
SCALING = 1.0 / math.sqrt(HD)
MESH = pl.DeviceIdType.MESH
VMEM_LIMIT = 56 * 1024 * 1024


def mm(a, b):
    return jnp.dot(a, b, preferred_element_type=jnp.float32)


def mm_nt(a, b):
    return lax.dot_general(a, b, (((1,), (1,)), ((), ())), preferred_element_type=jnp.float32)


def mm_tn(a, b):
    return lax.dot_general(a, b, (((0,), (0,)), ((), ())), preferred_element_type=jnp.float32)


def bf16(x):
    return x.astype(jnp.bfloat16)


def block_scale(ctx_place, row_count, b):
    first = ctx_place * row_count + b * BLOCK
    rows = lax.broadcasted_iota(jnp.int32, (BLOCK, HD), 0) + (first + 1)
    scale = 1.0 / (math.sqrt(HD) * jnp.sqrt(rows.astype(jnp.float32)))
    return scale


def causal_mask():
    u = lax.broadcasted_iota(jnp.int32, (BLOCK, BLOCK), 0)
    s = lax.broadcasted_iota(jnp.int32, (BLOCK, BLOCK), 1)
    return u >= s


def remote(src, dst, send, recv, target):
    return pltpu.make_async_remote_copy(
        src_ref=src, dst_ref=dst, send_sem=send, recv_sem=recv, device_id=target, device_id_type=MESH
    )


def enter(n_ctx, me, sib, par):
    barrier = pltpu.get_barrier_semaphore()
    for other in (sib, par):
        pl.semaphore_signal(barrier, inc=1, device_id={"head": other}, device_id_type=MESH)

    def greet(s, carry):
        to = lax.rem(me + s, n_ctx)
        pl.semaphore_signal(barrier, inc=1, device_id={"ctx": to}, device_id_type=MESH)
        return carry

    lax.fori_loop(1, n_ctx, greet, 0)
    pl.semaphore_wait(barrier, n_ctx + 1)


def asked(table, place, block, nblocks):
    count = jnp.int32(0)
    for i in range(nblocks):
        for r in range(LISTED):
            count = count + (table[place * nblocks + i, r] == block).astype(jnp.int32)
    return count


class Scan:
    def __init__(self, n_ctx, me, backward, own, total, out, arrived, send, recv):
        self.n_ctx, self.me, self.backward = n_ctx, me, backward
        self.own, self.total, self.out, self.arrived = own, total, out, arrived
        self.send, self.recv = send, recv
        self.steps = (n_ctx - 1).bit_length()

    def copy(self, i):
        shift = self.n_ctx - (1 << i) if self.backward else 1 << i
        to = lax.rem(self.me + shift, self.n_ctx)
        return remote(self.out.at[i], self.arrived.at[i], self.send.at[i], self.recv.at[i], {"ctx": to})

    def sends(self, i):
        return self.me >= (1 << i) if self.backward else self.me < self.n_ctx - (1 << i)

    def receives(self, i):
        return self.me < self.n_ctx - (1 << i) if self.backward else self.me >= (1 << i)

    def begin(self):
        self.total[...] = jnp.zeros_like(self.total)
        self.start(0)

    def start(self, i):
        self.out[i] = bf16(self.own[...] + self.total[...])

        @pl.when(self.sends(i))
        def _():
            self.copy(i).start()

    def receive(self, i):
        @pl.when(self.receives(i))
        def _():
            self.copy(i).wait_recv()
            self.total[...] += self.arrived[i].astype(jnp.float32)

    def advance(self, i):
        if i < self.steps:
            self.receive(i)
            if i + 1 < self.steps:
                self.start(i + 1)

    def finish(self):
        for i in range(self.steps):
            @pl.when(self.sends(i))
            def _():
                self.copy(i).wait_send()


def gather_kernel(
    n_ctx, table, q, k, v, og, w,
    g_out, lin_out, state_out, kv_in,
    og_sib, og_par, og_far, kv_out, st_blk, st_own, st_sum, st_out, st_in, total,
    sib_sems, par_send, par_recv, far_send, far_recv, kv_send, kv_recv, st_send, st_recv, own_sem,
):
    me = lax.axis_index("ctx")
    h = lax.axis_index("head")
    sib = h + 1 - 2 * lax.rem(h, 2)
    par = lax.rem(h + 2, 4)
    far = lax.rem(sib + 2, 4)
    rows, width = og.shape
    nblocks = rows // BLOCK
    chunks = rows // CHUNK
    enter(n_ctx, me, sib, par)

    def part(c):
        return pl.ds(pl.multiple_of(c * CHUNK, CHUNK), CHUNK)

    def par_copy(c):
        return remote(og.at[part(c)], og_par.at[part(c)], par_send.at[c], par_recv.at[c], {"head": par})

    def far_copy(c):
        return remote(og_par.at[part(c)], og_far.at[part(c)], far_send.at[c], far_recv.at[c], {"head": sib})

    sib_copy = remote(og, og_sib, sib_sems.at[0], sib_sems.at[1], {"head": sib})

    def kv_copy(s):
        to = lax.rem(me + s, n_ctx)
        return remote(kv_out.at[s], kv_in.at[me], kv_send.at[s], kv_recv.at[s], {"ctx": to})

    scan = Scan(n_ctx, me, False, st_own, st_sum, st_out, st_in, st_send, st_recv)

    def loop(first, last, step):
        def body(i, carry):
            step(i)
            return carry

        lax.fori_loop(first, last, body, 0)

    loop(0, chunks, lambda c: par_copy(c).start())

    def fill(s):
        to = lax.rem(me + s, n_ctx)
        picked_k = jnp.zeros((BLOCK, HD), jnp.float32)
        picked_v = jnp.zeros((BLOCK, HD), jnp.float32)
        for b in range(nblocks):
            here = slice(b * BLOCK, (b + 1) * BLOCK)
            chosen = asked(table, to, me * nblocks + b, nblocks).astype(jnp.float32)
            picked_k = picked_k + chosen * k[here, LIN_DEV * HD:].astype(jnp.float32)
            picked_v = picked_v + chosen * v[here, LIN_DEV * HD:].astype(jnp.float32)
        kv_out[s, :, :HD] = bf16(picked_k)
        kv_out[s, :, HD:] = bf16(picked_v)

    def fill_send(s):
        fill(s)
        kv_copy(s).start()

    loop(1, n_ctx, fill_send)
    sib_copy.start()
    fill(0)
    own_copy = pltpu.make_async_copy(kv_out.at[0], kv_in.at[me], own_sem)
    own_copy.start()

    for head in range(LIN_DEV):
        cols = slice(head * HD, (head + 1) * HD)
        device_state = jnp.zeros((HD, HD), jnp.float32)
        for b in range(nblocks):
            here = slice(b * BLOCK, (b + 1) * BLOCK)
            state = mm_tn(k[here, cols], v[here, cols])
            st_blk[b, head] = state
            device_state = device_state + state
        st_own[head] = device_state
    scan.begin()

    own_rows = pl.ds(pl.multiple_of(h * width, width), width)

    def own_product(c):
        total[part(c)] = mm(og[part(c)], w[own_rows])

    loop(0, chunks, own_product)
    scan.advance(0)
    sib_rows = pl.ds(pl.multiple_of(sib * width, width), width)
    sib_copy.wait_recv()

    def sib_product(c):
        total[part(c)] += mm(og_sib[part(c)], w[sib_rows])

    loop(0, chunks, sib_product)
    for i in range(1, scan.steps):
        scan.advance(i)
    for head in range(LIN_DEV):
        state = st_sum[head]
        for b in range(nblocks):
            state_out[b, head] = bf16(state)
            state = state + st_blk[b, head]

    for b in range(nblocks):
        scale = block_scale(me, rows, b)
        here = slice(b * BLOCK, (b + 1) * BLOCK)
        for head in range(LIN_DEV):
            cols = slice(head * HD, (head + 1) * HD)
            scores = mm_nt(q[here, cols], k[here, cols])
            weights = bf16(jnp.where(causal_mask(), scale[:, :1] * scores, 0.0))
            inside = mm(weights, v[here, cols])
            across = mm(q[here, cols], state_out[b, head])
            lin_out[here, cols] = bf16(inside + scale * across)

    par_rows = pl.ds(pl.multiple_of(par * width, width), width)
    far_rows = pl.ds(pl.multiple_of(far * width, width), width)

    def forward(c):
        par_copy(c).wait_recv()
        far_copy(c).start()
        total[part(c)] += mm(og_par[part(c)], w[par_rows])

    loop(0, chunks, forward)

    def last(c):
        far_copy(c).wait_recv()
        g_out[part(c)] = bf16(total[part(c)] + mm(og_far[part(c)], w[far_rows]))

    loop(0, chunks, last)

    loop(1, n_ctx, lambda s: kv_copy(s).wait())
    scan.finish()

    def finish_chunk(c):
        par_copy(c).wait_send()
        far_copy(c).wait_send()

    loop(0, chunks, finish_chunk)
    sib_copy.wait_send()
    own_copy.wait()


def sparse_kernel(
    table, place, q, k, v, g, far0, far1, far2, far3,
    out, dq_out, dk_out, dv_out, pairs,
    probs, pair_buf, sems,
):
    b = pl.program_id(0)
    nblocks = pl.num_programs(0)
    here = place[0] * nblocks + b
    fars = (far0, far1, far2, far3)
    neg = jnp.float32(-jnp.inf)
    qb, kb, vb, gb = q[...], k[...], v[...], g[...]
    scores = jnp.where(causal_mask(), mm_nt(qb, kb), neg)
    probs[0] = scores
    peak = jnp.max(scores, axis=1, keepdims=True)
    for r in range(LISTED):
        bias = jnp.where(table[here, r] != here, jnp.float32(0.0), neg)
        scores = mm_nt(qb, fars[r][0, :, :HD]) + bias
        probs[r + 1] = scores
        peak = jnp.maximum(peak, jnp.max(scores, axis=1, keepdims=True))
    sums = jnp.zeros((BLOCK, 1), jnp.float32)
    for r in range(LISTED + 1):
        e = jnp.exp((probs[r] - peak) * SCALING)
        probs[r] = e
        sums = sums + jnp.sum(e, axis=1, keepdims=True)
    inv = 1.0 / sums
    result = jnp.zeros((BLOCK, HD), jnp.float32)
    for r in range(LISTED + 1):
        prob = probs[r] * inv
        probs[r] = prob
        weight = bf16(prob)
        val = vb if r == 0 else fars[r - 1][0, :, HD:]
        result = result + mm(weight, val)
        dv = mm_tn(weight, gb)
        if r == 0:
            dv_out[...] = dv
        else:
            pair_buf[r - 1, :, HD:] = bf16(dv)
    result = bf16(result)
    out[...] = result
    row_dot = jnp.sum(gb.astype(jnp.float32) * result.astype(jnp.float32), axis=1, keepdims=True)
    dq = jnp.zeros((BLOCK, HD), jnp.float32)
    for r in range(LISTED + 1):
        val = vb if r == 0 else fars[r - 1][0, :, HD:]
        key = kb if r == 0 else fars[r - 1][0, :, :HD]
        ds = bf16(probs[r] * (mm_nt(gb, val) - row_dot))
        dq = dq + mm(ds, key)
        dk = SCALING * mm_tn(ds, qb)
        if r == 0:
            dk_out[...] = dk
        else:
            pair_buf[r - 1, :, :HD] = bf16(dk)
    dq_out[...] = bf16(SCALING * dq)
    copies = [
        pltpu.make_async_copy(pair_buf.at[r], pairs.at[table[here, r] // nblocks], sems.at[r]) for r in range(LISTED)
    ]
    for copy in copies:
        copy.start()
    for copy in copies:
        copy.wait()


def scatter_kernel(
    n_ctx, table, q, k, v, g, w, lin, sp, state, dq_sp, dk_sp, dv_sp, pairs,
    layer, dq_out, dk_out, dv_out,
    ret, att, to_far, from_far, to_par, from_par, to_sib, from_sib, own, adj_blk, adj_own, adj_sum, adj_out, adj_in, adj,
    ret_send, ret_recv, adj_send, adj_recv, far_send, far_recv, par_send, par_recv, sib_send, sib_recv, own_sem,
):
    me = lax.axis_index("ctx")
    h = lax.axis_index("head")
    sib = h + 1 - 2 * lax.rem(h, 2)
    par = lax.rem(h + 2, 4)
    far = lax.rem(sib + 2, 4)
    rows, width = own.shape
    nblocks = rows // BLOCK
    chunks = rows // CHUNK
    enter(n_ctx, me, sib, par)

    def part(c):
        return pl.ds(pl.multiple_of(c * CHUNK, CHUNK), CHUNK)

    def loop(first, last, step):
        def body(i, carry):
            step(i)
            return carry

        lax.fori_loop(first, last, body, 0)

    def ret_copy(s):
        to = lax.rem(me + s, n_ctx)
        return remote(pairs.at[to], ret.at[me], ret_send.at[s], ret_recv.at[s], {"ctx": to})

    scan = Scan(n_ctx, me, True, adj_own, adj_sum, adj_out, adj_in, adj_send, adj_recv)

    def far_copy(c):
        return remote(to_far.at[part(c)], from_far.at[part(c)], far_send.at[c], far_recv.at[c], {"head": sib})

    def par_copy(c):
        return remote(to_par.at[part(c)], from_par.at[part(c)], par_send.at[c], par_recv.at[c], {"head": par})

    def sib_copy(c):
        return remote(to_sib.at[part(c)], from_sib.at[part(c)], sib_send.at[c], sib_recv.at[c], {"head": sib})

    loop(1, n_ctx, lambda s: ret_copy(s).start())
    own_copy = pltpu.make_async_copy(pairs.at[me], ret.at[me], own_sem)
    own_copy.start()
    att[:, :LIN_DEV * HD] = lin[...]
    att[:, LIN_DEV * HD:] = sp[...]

    def product(c, dest):
        return mm_nt(att[part(c)], w[pl.ds(pl.multiple_of(dest * width, width), width)])

    def far_step(c):
        to_far[part(c)] = bf16(product(c, far))
        far_copy(c).start()

    loop(0, chunks, far_step)

    for head in range(LIN_DEV):
        cols = slice(head * HD, (head + 1) * HD)
        device_adj = jnp.zeros((HD, HD), jnp.float32)
        for b in range(nblocks):
            here = slice(b * BLOCK, (b + 1) * BLOCK)
            scaled = bf16(block_scale(me, rows, b) * g[here, cols].astype(jnp.float32))
            one = mm_tn(q[here, cols], scaled)
            adj_blk[b, head] = one
            device_adj = device_adj + one
        adj_own[head] = device_adj
    scan.begin()

    def par_step(c):
        mine = product(c, par)
        far_copy(c).wait_recv()
        to_par[part(c)] = bf16(mine + from_far[part(c)].astype(jnp.float32))
        par_copy(c).start()

    loop(0, chunks, par_step)

    scan.advance(0)

    def sib_step(c):
        to_sib[part(c)] = bf16(product(c, sib))
        sib_copy(c).start()

    loop(0, chunks, sib_step)
    scan.advance(1)

    def own_step(c):
        own[part(c)] = product(c, h)

    loop(0, chunks, own_step)

    for i in range(2, scan.steps):
        scan.advance(i)
    for head in range(LIN_DEV):
        total = adj_sum[head]
        for b in reversed(range(nblocks)):
            adj[b, head] = bf16(total)
            total = total + adj_blk[b, head]

    for b in range(nblocks):
        scale = block_scale(me, rows, b)
        here = slice(b * BLOCK, (b + 1) * BLOCK)
        for head in range(LIN_DEV):
            cols = slice(head * HD, (head + 1) * HD)
            qb, kb, vb, gb = q[here, cols], k[here, cols], v[here, cols], g[here, cols]
            keep = causal_mask()
            weights = bf16(jnp.where(keep, scale[:, :1] * mm_nt(qb, kb), 0.0))
            grads = bf16(jnp.where(keep, scale[:, :1] * mm_nt(gb, vb), 0.0))
            dq_out[here, cols] = bf16(mm(grads, kb) + scale * mm_nt(gb, state[b, head]))
            dk_out[here, cols] = bf16(mm_tn(grads, qb) + mm_nt(vb, adj[b, head]))
            dv_out[here, cols] = bf16(mm_tn(weights, gb) + mm(kb, adj[b, head]))
        dq_out[here, LIN_DEV * HD:] = dq_sp[here]

    own_copy.wait()
    loop(1, n_ctx, lambda s: ret_copy(s).wait())
    last = slice(LIN_DEV * HD, (LIN_DEV + 1) * HD)
    for b in range(nblocks):
        for t in range(BLOCK // HD):
            here = slice(t * HD, (t + 1) * HD)
            place = slice(b * BLOCK + t * HD, b * BLOCK + (t + 1) * HD)

            def add(j, sums):
                mine = jnp.full((1, 2 * HD), asked(table, j, me * nblocks + b, nblocks), jnp.int32) > 0
                got = ret[j, here].astype(jnp.float32)
                return sums + jnp.where(mine, got, 0.0)

            sums = lax.fori_loop(0, n_ctx, add, jnp.zeros((HD, 2 * HD), jnp.float32))
            dk_out[place, last] = bf16(dk_sp[place] + sums[:, :HD])
            dv_out[place, last] = bf16(dv_sp[place] + sums[:, HD:])

    def final(c):
        sib_copy(c).wait()
        par_copy(c).wait()
        far_copy(c).wait_send()
        layer[part(c)] = bf16(
            own[part(c)] + from_sib[part(c)].astype(jnp.float32) + from_par[part(c)].astype(jnp.float32)
        )

    loop(0, chunks, final)
    scan.finish()


def local(queries, keys, values, out_weight, out_grad, long_blocks):
    rows = queries.shape[0]
    nblocks = rows // BLOCK
    n_ctx = lax.axis_size("ctx")
    place = lax.axis_index("ctx").astype(jnp.int32).reshape(1)
    width = out_grad.shape[1]
    chunks = rows // CHUNK
    wide = LIN_DEV * HD
    steps = (n_ctx - 1).bit_length()

    smem = pl.BlockSpec(memory_space=pltpu.SMEM)
    vmem = pl.BlockSpec(memory_space=pltpu.VMEM)
    anywhere = pl.BlockSpec(memory_space=pl.ANY)
    b16, f32 = jnp.bfloat16, jnp.float32
    dma = pltpu.SemaphoreType.DMA

    attn_grad, lin_out, state, kv_in = pl.pallas_call(
        functools.partial(gather_kernel, n_ctx),
        name="gather",
        out_shape=(
            jax.ShapeDtypeStruct((rows, wide + HD), b16),
            jax.ShapeDtypeStruct((rows, wide), b16),
            jax.ShapeDtypeStruct((nblocks, LIN_DEV, HD, HD), b16),
            jax.ShapeDtypeStruct((n_ctx, BLOCK, 2 * HD), b16),
        ),
        in_specs=[smem] + [vmem] * 5,
        out_specs=(vmem, vmem, vmem, anywhere),
        scratch_shapes=[
            pltpu.VMEM((rows, width), b16),
            pltpu.VMEM((rows, width), b16),
            pltpu.VMEM((rows, width), b16),
            pltpu.VMEM((n_ctx, BLOCK, 2 * HD), b16),
            pltpu.VMEM((nblocks, LIN_DEV, HD, HD), f32),
            pltpu.VMEM((LIN_DEV, HD, HD), f32),
            pltpu.VMEM((LIN_DEV, HD, HD), f32),
            pltpu.VMEM((steps, LIN_DEV, HD, HD), b16),
            pltpu.VMEM((steps, LIN_DEV, HD, HD), b16),
            pltpu.VMEM((rows, wide + HD), f32),
            dma((2,)),
            dma((chunks,)),
            dma((chunks,)),
            dma((chunks,)),
            dma((chunks,)),
            dma((n_ctx,)),
            dma((n_ctx,)),
            dma((steps,)),
            dma((steps,)),
            dma(()),
        ],
        compiler_params=pltpu.CompilerParams(
            collective_id=0, has_side_effects=True, vmem_limit_bytes=VMEM_LIMIT
        ),
    )(long_blocks, queries, keys, values, out_grad, out_weight)

    column = pl.BlockSpec((BLOCK, HD), lambda b, table, place: (b, LIN_DEV))
    single = pl.BlockSpec((BLOCK, HD), lambda b, table, place: (b, 0))

    def far_spec(r):
        return pl.BlockSpec((1, BLOCK, 2 * HD), lambda b, table, place: (table[place[0] * nblocks + b, r] // nblocks, 0, 0))

    sparse_out, dq_sp, dk_sp, dv_sp, pairs = pl.pallas_call(
        sparse_kernel,
        name="sparse",
        out_shape=(
            jax.ShapeDtypeStruct((rows, HD), b16),
            jax.ShapeDtypeStruct((rows, HD), b16),
            jax.ShapeDtypeStruct((rows, HD), f32),
            jax.ShapeDtypeStruct((rows, HD), f32),
            jax.ShapeDtypeStruct((n_ctx, BLOCK, 2 * HD), b16),
        ),
        grid_spec=pltpu.PrefetchScalarGridSpec(
            num_scalar_prefetch=2,
            grid=(nblocks,),
            in_specs=[column] * 4 + [far_spec(r) for r in range(LISTED)],
            out_specs=(single, single, single, single, anywhere),
            scratch_shapes=[
                pltpu.VMEM((LISTED + 1, BLOCK, BLOCK), f32),
                pltpu.VMEM((LISTED, BLOCK, 2 * HD), b16),
                dma((LISTED,)),
            ],
        ),
        compiler_params=pltpu.CompilerParams(vmem_limit_bytes=VMEM_LIMIT),
    )(long_blocks, place, queries, keys, values, attn_grad, kv_in, kv_in, kv_in, kv_in)

    big = pltpu.VMEM((rows, width), b16)
    return pl.pallas_call(
        functools.partial(scatter_kernel, n_ctx),
        name="scatter",
        out_shape=(
            jax.ShapeDtypeStruct((rows, width), b16),
            jax.ShapeDtypeStruct((rows, wide + HD), b16),
            jax.ShapeDtypeStruct((rows, wide + HD), b16),
            jax.ShapeDtypeStruct((rows, wide + HD), b16),
        ),
        in_specs=[smem] + [vmem] * 11 + [anywhere],
        out_specs=(vmem, vmem, vmem, vmem),
        scratch_shapes=[
            pltpu.VMEM((n_ctx, BLOCK, 2 * HD), b16),
            pltpu.VMEM((rows, wide + HD), b16),
            big, big, big, big, big, big,
            pltpu.VMEM((rows, width), f32),
            pltpu.VMEM((nblocks, LIN_DEV, HD, HD), f32),
            pltpu.VMEM((LIN_DEV, HD, HD), f32),
            pltpu.VMEM((LIN_DEV, HD, HD), f32),
            pltpu.VMEM((steps, LIN_DEV, HD, HD), b16),
            pltpu.VMEM((steps, LIN_DEV, HD, HD), b16),
            pltpu.VMEM((nblocks, LIN_DEV, HD, HD), b16),
            dma((n_ctx,)),
            dma((n_ctx,)),
            dma((steps,)),
            dma((steps,)),
            dma((chunks,)),
            dma((chunks,)),
            dma((chunks,)),
            dma((chunks,)),
            dma((chunks,)),
            dma((chunks,)),
            dma(()),
        ],
        compiler_params=pltpu.CompilerParams(
            collective_id=1, has_side_effects=True, vmem_limit_bytes=VMEM_LIMIT
        ),
    )(
        long_blocks, queries, keys, values, attn_grad, out_weight, lin_out, sparse_out, state,
        dq_sp, dk_sp, dv_sp, pairs,
    )


def solution(mesh):
    return jax.shard_map(
        local,
        mesh=mesh,
        in_specs=(
            P("ctx", "head"),
            P("ctx", "head"),
            P("ctx", "head"),
            P(None, "head"),
            P("ctx", "head"),
            P(),
        ),
        out_specs=(P("ctx", "head"), P("ctx", "head"), P("ctx", "head"), P("ctx", "head")),
        check_vma=False,
    )
```

```python
import functools
import math

import jax
import jax.numpy as jnp
from jax import lax
from jax.experimental import pallas as pl
from jax.experimental.pallas import tpu as pltpu
from jax.sharding import PartitionSpec as P

HD = 128
LIN_DEV = 3
LISTED = 4
BLOCK = 512
CHUNK = 256
SCALING = 1.0 / math.sqrt(HD)
MESH = pl.DeviceIdType.MESH
VMEM_LIMIT = 56 * 1024 * 1024


def mm(a, b):
    return jnp.dot(a, b, preferred_element_type=jnp.float32)


def mm_nt(a, b):
    return lax.dot_general(a, b, (((1,), (1,)), ((), ())), preferred_element_type=jnp.float32)


def mm_tn(a, b):
    return lax.dot_general(a, b, (((0,), (0,)), ((), ())), preferred_element_type=jnp.float32)


def bf16(x):
    return x.astype(jnp.bfloat16)


def block_scale(ctx_place, row_count, b):
    first = ctx_place * row_count + b * BLOCK
    rows = lax.broadcasted_iota(jnp.int32, (BLOCK, HD), 0) + (first + 1)
    scale = 1.0 / (math.sqrt(HD) * jnp.sqrt(rows.astype(jnp.float32)))
    return scale


def causal_mask():
    u = lax.broadcasted_iota(jnp.int32, (BLOCK, BLOCK), 0)
    s = lax.broadcasted_iota(jnp.int32, (BLOCK, BLOCK), 1)
    return u >= s


def remote(src, dst, send, recv, target):
    return pltpu.make_async_remote_copy(
        src_ref=src, dst_ref=dst, send_sem=send, recv_sem=recv, device_id=target, device_id_type=MESH
    )


def enter(n_ctx, me, sib, par):
    barrier = pltpu.get_barrier_semaphore()
    for other in (sib, par):
        pl.semaphore_signal(barrier, inc=1, device_id={"head": other}, device_id_type=MESH)

    def greet(s, carry):
        to = lax.rem(me + s, n_ctx)
        pl.semaphore_signal(barrier, inc=1, device_id={"ctx": to}, device_id_type=MESH)
        return carry

    lax.fori_loop(1, n_ctx, greet, 0)
    pl.semaphore_wait(barrier, n_ctx + 1)


def asked(table, place, block, nblocks):
    count = jnp.int32(0)
    for i in range(nblocks):
        for r in range(LISTED):
            count = count + (table[place * nblocks + i, r] == block).astype(jnp.int32)
    return count


class Scan:
    def __init__(self, n_ctx, me, backward, own, total, out, arrived, send, recv):
        self.n_ctx, self.me, self.backward = n_ctx, me, backward
        self.own, self.total, self.out, self.arrived = own, total, out, arrived
        self.send, self.recv = send, recv
        self.steps = (n_ctx - 1).bit_length()

    def copy(self, i):
        shift = self.n_ctx - (1 << i) if self.backward else 1 << i
        to = lax.rem(self.me + shift, self.n_ctx)
        return remote(self.out.at[i], self.arrived.at[i], self.send.at[i], self.recv.at[i], {"ctx": to})

    def sends(self, i):
        return self.me >= (1 << i) if self.backward else self.me < self.n_ctx - (1 << i)

    def receives(self, i):
        return self.me < self.n_ctx - (1 << i) if self.backward else self.me >= (1 << i)

    def begin(self):
        self.total[...] = jnp.zeros_like(self.total)
        self.start(0)

    def start(self, i):
        self.out[i] = bf16(self.own[...] + self.total[...])

        @pl.when(self.sends(i))
        def _():
            self.copy(i).start()

    def receive(self, i):
        @pl.when(self.receives(i))
        def _():
            self.copy(i).wait_recv()
            self.total[...] += self.arrived[i].astype(jnp.float32)

    def advance(self, i):
        if i < self.steps:
            self.receive(i)
            if i + 1 < self.steps:
                self.start(i + 1)

    def finish(self):
        for i in range(self.steps):
            @pl.when(self.sends(i))
            def _():
                self.copy(i).wait_send()


def gather_kernel(
    n_ctx, table, q, k, v, og, w,
    g_out, lin_out, state_out, kv_in,
    og_sib, og_par, og_far, kv_out, lin_acc, st_blk, st_own, st_sum, st_out, st_in, total,
    sib_sems, par_send, par_recv, far_send, far_recv, kv_send, kv_recv, st_send, st_recv, own_sem,
):
    me = lax.axis_index("ctx")
    h = lax.axis_index("head")
    sib = h + 1 - 2 * lax.rem(h, 2)
    par = lax.rem(h + 2, 4)
    far = lax.rem(sib + 2, 4)
    rows, width = og.shape
    nblocks = rows // BLOCK
    chunks = rows // CHUNK
    enter(n_ctx, me, sib, par)

    def part(c):
        return pl.ds(pl.multiple_of(c * CHUNK, CHUNK), CHUNK)

    def par_copy(c):
        return remote(og.at[part(c)], og_par.at[part(c)], par_send.at[c], par_recv.at[c], {"head": par})

    def far_copy(c):
        return remote(og_par.at[part(c)], og_far.at[part(c)], far_send.at[c], far_recv.at[c], {"head": sib})

    sib_copy = remote(og, og_sib, sib_sems.at[0], sib_sems.at[1], {"head": sib})

    def kv_copy(s):
        to = lax.rem(me + s, n_ctx)
        return remote(kv_out.at[s], kv_in.at[me], kv_send.at[s], kv_recv.at[s], {"ctx": to})

    scan = Scan(n_ctx, me, False, st_own, st_sum, st_out, st_in, st_send, st_recv)

    def loop(first, last, step):
        def body(i, carry):
            step(i)
            return carry

        lax.fori_loop(first, last, body, 0)

    loop(0, chunks, lambda c: par_copy(c).start())

    def fill(s):
        to = lax.rem(me + s, n_ctx)
        picked_k = jnp.zeros((BLOCK, HD), jnp.float32)
        picked_v = jnp.zeros((BLOCK, HD), jnp.float32)
        for b in range(nblocks):
            here = slice(b * BLOCK, (b + 1) * BLOCK)
            chosen = asked(table, to, me * nblocks + b, nblocks).astype(jnp.float32)
            picked_k = picked_k + chosen * k[here, LIN_DEV * HD:].astype(jnp.float32)
            picked_v = picked_v + chosen * v[here, LIN_DEV * HD:].astype(jnp.float32)
        kv_out[s, :, :HD] = bf16(picked_k)
        kv_out[s, :, HD:] = bf16(picked_v)

    def fill_send(s):
        fill(s)
        kv_copy(s).start()

    for head in range(LIN_DEV):
        cols = slice(head * HD, (head + 1) * HD)
        device_state = jnp.zeros((HD, HD), jnp.float32)
        for b in range(nblocks):
            here = slice(b * BLOCK, (b + 1) * BLOCK)
            state = mm_tn(k[here, cols], v[here, cols])
            st_blk[b, head] = state
            device_state = device_state + state
        st_own[head] = device_state
    scan.begin()
    loop(1, n_ctx, fill_send)
    sib_copy.start()
    fill(0)
    own_copy = pltpu.make_async_copy(kv_out.at[0], kv_in.at[me], own_sem)
    own_copy.start()

    own_rows = pl.ds(pl.multiple_of(h * width, width), width)

    def own_product(c):
        total[part(c)] = mm(og[part(c)], w[own_rows])

    loop(0, chunks, own_product)
    scan.advance(0)
    sib_rows = pl.ds(pl.multiple_of(sib * width, width), width)
    sib_copy.wait_recv()

    def sib_product(c):
        total[part(c)] += mm(og_sib[part(c)], w[sib_rows])

    loop(0, chunks, sib_product)
    for b in range(nblocks):
        scale = block_scale(me, rows, b)
        here = slice(b * BLOCK, (b + 1) * BLOCK)
        for head in range(LIN_DEV):
            cols = slice(head * HD, (head + 1) * HD)
            scores = mm_nt(q[here, cols], k[here, cols])
            weights = bf16(jnp.where(causal_mask(), scale[:, :1] * scores, 0.0))
            inside = mm(weights, v[here, cols])
            lin_acc[here, cols] = inside

    par_rows = pl.ds(pl.multiple_of(par * width, width), width)
    far_rows = pl.ds(pl.multiple_of(far * width, width), width)

    def forward(c):
        par_copy(c).wait_recv()
        far_copy(c).start()
        total[part(c)] += mm(og_par[part(c)], w[par_rows])

    loop(0, chunks // 2, forward)
    scan.advance(1)
    loop(chunks // 2, chunks, forward)
    for i in range(2, scan.steps):
        scan.advance(i)
    for head in range(LIN_DEV):
        state = st_sum[head]
        for b in range(nblocks):
            state_out[b, head] = bf16(state)
            state = state + st_blk[b, head]

    for b in range(nblocks):
        scale = block_scale(me, rows, b)
        here = slice(b * BLOCK, (b + 1) * BLOCK)
        for head in range(LIN_DEV):
            cols = slice(head * HD, (head + 1) * HD)
            across = mm(q[here, cols], state_out[b, head])
            lin_out[here, cols] = bf16(lin_acc[here, cols] + scale * across)


    def last(c):
        far_copy(c).wait_recv()
        g_out[part(c)] = bf16(total[part(c)] + mm(og_far[part(c)], w[far_rows]))

    loop(0, chunks, last)

    loop(1, n_ctx, lambda s: kv_copy(s).wait())
    scan.finish()

    def finish_chunk(c):
        par_copy(c).wait_send()
        far_copy(c).wait_send()

    loop(0, chunks, finish_chunk)
    sib_copy.wait_send()
    own_copy.wait()


def sparse_kernel(
    table, place, q, k, v, g, far0, far1, far2, far3,
    out, dq_out, dk_out, dv_out, pairs,
    probs, pair_buf, sems,
):
    b = pl.program_id(0)
    nblocks = pl.num_programs(0)
    here = place[0] * nblocks + b
    fars = (far0, far1, far2, far3)
    neg = jnp.float32(-jnp.inf)
    qb, kb, vb, gb = q[...], k[...], v[...], g[...]
    scores = jnp.where(causal_mask(), mm_nt(qb, kb), neg)
    probs[0] = scores
    peak = jnp.max(scores, axis=1, keepdims=True)
    for r in range(LISTED):
        bias = jnp.where(table[here, r] != here, jnp.float32(0.0), neg)
        scores = mm_nt(qb, fars[r][0, :, :HD]) + bias
        probs[r + 1] = scores
        peak = jnp.maximum(peak, jnp.max(scores, axis=1, keepdims=True))
    sums = jnp.zeros((BLOCK, 1), jnp.float32)
    for r in range(LISTED + 1):
        e = jnp.exp((probs[r] - peak) * SCALING)
        probs[r] = e
        sums = sums + jnp.sum(e, axis=1, keepdims=True)
    inv = 1.0 / sums
    result = jnp.zeros((BLOCK, HD), jnp.float32)
    for r in range(LISTED + 1):
        prob = probs[r] * inv
        probs[r] = prob
        weight = bf16(prob)
        val = vb if r == 0 else fars[r - 1][0, :, HD:]
        result = result + mm(weight, val)
        dv = mm_tn(weight, gb)
        if r == 0:
            dv_out[...] = dv
        else:
            pair_buf[r - 1, :, HD:] = bf16(dv)
    result = bf16(result)
    out[...] = result
    row_dot = jnp.sum(gb.astype(jnp.float32) * result.astype(jnp.float32), axis=1, keepdims=True)
    dq = jnp.zeros((BLOCK, HD), jnp.float32)
    for r in range(LISTED + 1):
        val = vb if r == 0 else fars[r - 1][0, :, HD:]
        key = kb if r == 0 else fars[r - 1][0, :, :HD]
        ds = bf16(probs[r] * (mm_nt(gb, val) - row_dot))
        dq = dq + mm(ds, key)
        dk = SCALING * mm_tn(ds, qb)
        if r == 0:
            dk_out[...] = dk
        else:
            pair_buf[r - 1, :, :HD] = bf16(dk)
    dq_out[...] = bf16(SCALING * dq)
    copies = [
        pltpu.make_async_copy(pair_buf.at[r], pairs.at[table[here, r] // nblocks], sems.at[r]) for r in range(LISTED)
    ]
    for copy in copies:
        copy.start()
    for copy in copies:
        copy.wait()


def scatter_kernel(
    n_ctx, table, q, k, v, g, w, lin, sp, state, dq_sp, dk_sp, dv_sp, pairs,
    layer, dq_out, dk_out, dv_out,
    ret, att, to_far, from_far, to_par, from_par, to_sib, from_sib, own, dk_acc, dv_acc, adj_blk, adj_own, adj_sum, adj_out, adj_in, adj,
    ret_send, ret_recv, adj_send, adj_recv, far_send, far_recv, par_send, par_recv, sib_send, sib_recv, own_sem,
):
    me = lax.axis_index("ctx")
    h = lax.axis_index("head")
    sib = h + 1 - 2 * lax.rem(h, 2)
    par = lax.rem(h + 2, 4)
    far = lax.rem(sib + 2, 4)
    rows, width = own.shape
    nblocks = rows // BLOCK
    chunks = rows // CHUNK
    enter(n_ctx, me, sib, par)

    def part(c):
        return pl.ds(pl.multiple_of(c * CHUNK, CHUNK), CHUNK)

    def loop(first, last, step):
        def body(i, carry):
            step(i)
            return carry

        lax.fori_loop(first, last, body, 0)

    def ret_copy(s):
        to = lax.rem(me + s, n_ctx)
        return remote(pairs.at[to], ret.at[me], ret_send.at[s], ret_recv.at[s], {"ctx": to})

    scan = Scan(n_ctx, me, True, adj_own, adj_sum, adj_out, adj_in, adj_send, adj_recv)

    def far_copy(c):
        return remote(to_far.at[part(c)], from_far.at[part(c)], far_send.at[c], far_recv.at[c], {"head": sib})

    def par_copy(c):
        return remote(to_par.at[part(c)], from_par.at[part(c)], par_send.at[c], par_recv.at[c], {"head": par})

    def sib_copy(c):
        return remote(to_sib.at[part(c)], from_sib.at[part(c)], sib_send.at[c], sib_recv.at[c], {"head": sib})

    for head in range(LIN_DEV):
        cols = slice(head * HD, (head + 1) * HD)
        device_adj = jnp.zeros((HD, HD), jnp.float32)
        for b in range(nblocks):
            here = slice(b * BLOCK, (b + 1) * BLOCK)
            scaled = bf16(block_scale(me, rows, b) * g[here, cols].astype(jnp.float32))
            one = mm_tn(q[here, cols], scaled)
            adj_blk[b, head] = one
            device_adj = device_adj + one
        adj_own[head] = device_adj
    scan.begin()
    loop(1, n_ctx, lambda s: ret_copy(s).start())
    own_copy = pltpu.make_async_copy(pairs.at[me], ret.at[me], own_sem)
    own_copy.start()
    att[:, :LIN_DEV * HD] = lin[...]
    att[:, LIN_DEV * HD:] = sp[...]

    def product(c, dest):
        return mm_nt(att[part(c)], w[pl.ds(pl.multiple_of(dest * width, width), width)])

    def far_step(c):
        to_far[part(c)] = bf16(product(c, far))
        far_copy(c).start()

    loop(0, chunks, far_step)

    def par_step(c):
        mine = product(c, par)
        far_copy(c).wait_recv()
        to_par[part(c)] = bf16(mine + from_far[part(c)].astype(jnp.float32))
        par_copy(c).start()

    loop(0, chunks, par_step)

    scan.advance(0)

    def sib_step(c):
        to_sib[part(c)] = bf16(product(c, sib))
        sib_copy(c).start()

    loop(0, chunks, sib_step)

    def own_step(c):
        own[part(c)] = product(c, h)

    loop(0, chunks, own_step)
    scan.advance(1)

    for b in range(nblocks):
        scale = block_scale(me, rows, b)
        here = slice(b * BLOCK, (b + 1) * BLOCK)
        for head in range(LIN_DEV):
            cols = slice(head * HD, (head + 1) * HD)
            qb, kb, vb, gb = q[here, cols], k[here, cols], v[here, cols], g[here, cols]
            keep = causal_mask()
            weights = bf16(jnp.where(keep, scale[:, :1] * mm_nt(qb, kb), 0.0))
            grads = bf16(jnp.where(keep, scale[:, :1] * mm_nt(gb, vb), 0.0))
            dq_out[here, cols] = bf16(mm(grads, kb) + scale * mm_nt(gb, state[b, head]))
            dk_acc[here, cols] = mm_tn(grads, qb)
            dv_acc[here, cols] = mm_tn(weights, gb)
        dq_out[here, LIN_DEV * HD:] = dq_sp[here]

    own_copy.wait()
    loop(1, n_ctx, lambda s: ret_copy(s).wait())
    last = slice(LIN_DEV * HD, (LIN_DEV + 1) * HD)
    for b in range(nblocks):
        for t in range(BLOCK // HD):
            here = slice(t * HD, (t + 1) * HD)
            place = slice(b * BLOCK + t * HD, b * BLOCK + (t + 1) * HD)

            def add(j, sums):
                mine = jnp.full((1, 2 * HD), asked(table, j, me * nblocks + b, nblocks), jnp.int32) > 0
                got = ret[j, here].astype(jnp.float32)
                return sums + jnp.where(mine, got, 0.0)

            sums = lax.fori_loop(0, n_ctx, add, jnp.zeros((HD, 2 * HD), jnp.float32))
            dk_out[place, last] = bf16(dk_sp[place] + sums[:, :HD])
            dv_out[place, last] = bf16(dv_sp[place] + sums[:, HD:])

    def final(c):
        sib_copy(c).wait()
        par_copy(c).wait()
        far_copy(c).wait_send()
        layer[part(c)] = bf16(
            own[part(c)] + from_sib[part(c)].astype(jnp.float32) + from_par[part(c)].astype(jnp.float32)
        )

    loop(0, chunks, final)
    for i in range(2, scan.steps):
        scan.advance(i)
    for head in range(LIN_DEV):
        total = adj_sum[head]
        for b in reversed(range(nblocks)):
            adj[b, head] = bf16(total)
            total = total + adj_blk[b, head]

    for b in range(nblocks):
        here = slice(b * BLOCK, (b + 1) * BLOCK)
        for head in range(LIN_DEV):
            cols = slice(head * HD, (head + 1) * HD)
            dk_out[here, cols] = bf16(dk_acc[here, cols] + mm_nt(v[here, cols], adj[b, head]))
            dv_out[here, cols] = bf16(dv_acc[here, cols] + mm(k[here, cols], adj[b, head]))
    scan.finish()


def local(queries, keys, values, out_weight, out_grad, long_blocks):
    rows = queries.shape[0]
    nblocks = rows // BLOCK
    n_ctx = lax.axis_size("ctx")
    place = lax.axis_index("ctx").astype(jnp.int32).reshape(1)
    width = out_grad.shape[1]
    chunks = rows // CHUNK
    wide = LIN_DEV * HD
    steps = (n_ctx - 1).bit_length()

    smem = pl.BlockSpec(memory_space=pltpu.SMEM)
    vmem = pl.BlockSpec(memory_space=pltpu.VMEM)
    anywhere = pl.BlockSpec(memory_space=pl.ANY)
    b16, f32 = jnp.bfloat16, jnp.float32
    dma = pltpu.SemaphoreType.DMA

    attn_grad, lin_out, state, kv_in = pl.pallas_call(
        functools.partial(gather_kernel, n_ctx),
        name="gather",
        out_shape=(
            jax.ShapeDtypeStruct((rows, wide + HD), b16),
            jax.ShapeDtypeStruct((rows, wide), b16),
            jax.ShapeDtypeStruct((nblocks, LIN_DEV, HD, HD), b16),
            jax.ShapeDtypeStruct((n_ctx, BLOCK, 2 * HD), b16),
        ),
        in_specs=[smem] + [vmem] * 5,
        out_specs=(vmem, vmem, vmem, anywhere),
        scratch_shapes=[
            pltpu.VMEM((rows, width), b16),
            pltpu.VMEM((rows, width), b16),
            pltpu.VMEM((rows, width), b16),
            pltpu.VMEM((n_ctx, BLOCK, 2 * HD), b16),
            pltpu.VMEM((rows, wide), f32),
            pltpu.VMEM((nblocks, LIN_DEV, HD, HD), f32),
            pltpu.VMEM((LIN_DEV, HD, HD), f32),
            pltpu.VMEM((LIN_DEV, HD, HD), f32),
            pltpu.VMEM((steps, LIN_DEV, HD, HD), b16),
            pltpu.VMEM((steps, LIN_DEV, HD, HD), b16),
            pltpu.VMEM((rows, wide + HD), f32),
            dma((2,)),
            dma((chunks,)),
            dma((chunks,)),
            dma((chunks,)),
            dma((chunks,)),
            dma((n_ctx,)),
            dma((n_ctx,)),
            dma((steps,)),
            dma((steps,)),
            dma(()),
        ],
        compiler_params=pltpu.CompilerParams(
            collective_id=0, has_side_effects=True, vmem_limit_bytes=VMEM_LIMIT
        ),
    )(long_blocks, queries, keys, values, out_grad, out_weight)

    column = pl.BlockSpec((BLOCK, HD), lambda b, table, place: (b, LIN_DEV))
    single = pl.BlockSpec((BLOCK, HD), lambda b, table, place: (b, 0))

    def far_spec(r):
        return pl.BlockSpec((1, BLOCK, 2 * HD), lambda b, table, place: (table[place[0] * nblocks + b, r] // nblocks, 0, 0))

    sparse_out, dq_sp, dk_sp, dv_sp, pairs = pl.pallas_call(
        sparse_kernel,
        name="sparse",
        out_shape=(
            jax.ShapeDtypeStruct((rows, HD), b16),
            jax.ShapeDtypeStruct((rows, HD), b16),
            jax.ShapeDtypeStruct((rows, HD), f32),
            jax.ShapeDtypeStruct((rows, HD), f32),
            jax.ShapeDtypeStruct((n_ctx, BLOCK, 2 * HD), b16),
        ),
        grid_spec=pltpu.PrefetchScalarGridSpec(
            num_scalar_prefetch=2,
            grid=(nblocks,),
            in_specs=[column] * 4 + [far_spec(r) for r in range(LISTED)],
            out_specs=(single, single, single, single, anywhere),
            scratch_shapes=[
                pltpu.VMEM((LISTED + 1, BLOCK, BLOCK), f32),
                pltpu.VMEM((LISTED, BLOCK, 2 * HD), b16),
                dma((LISTED,)),
            ],
        ),
        compiler_params=pltpu.CompilerParams(vmem_limit_bytes=VMEM_LIMIT),
    )(long_blocks, place, queries, keys, values, attn_grad, kv_in, kv_in, kv_in, kv_in)

    big = pltpu.VMEM((rows, width), b16)
    return pl.pallas_call(
        functools.partial(scatter_kernel, n_ctx),
        name="scatter",
        out_shape=(
            jax.ShapeDtypeStruct((rows, width), b16),
            jax.ShapeDtypeStruct((rows, wide + HD), b16),
            jax.ShapeDtypeStruct((rows, wide + HD), b16),
            jax.ShapeDtypeStruct((rows, wide + HD), b16),
        ),
        in_specs=[smem] + [vmem] * 11 + [anywhere],
        out_specs=(vmem, vmem, vmem, vmem),
        scratch_shapes=[
            pltpu.VMEM((n_ctx, BLOCK, 2 * HD), b16),
            pltpu.VMEM((rows, wide + HD), b16),
            big, big, big, big, big, big,
            pltpu.VMEM((rows, width), f32),
            pltpu.VMEM((rows, wide), f32),
            pltpu.VMEM((rows, wide), f32),
            pltpu.VMEM((nblocks, LIN_DEV, HD, HD), f32),
            pltpu.VMEM((LIN_DEV, HD, HD), f32),
            pltpu.VMEM((LIN_DEV, HD, HD), f32),
            pltpu.VMEM((steps, LIN_DEV, HD, HD), b16),
            pltpu.VMEM((steps, LIN_DEV, HD, HD), b16),
            pltpu.VMEM((nblocks, LIN_DEV, HD, HD), b16),
            dma((n_ctx,)),
            dma((n_ctx,)),
            dma((steps,)),
            dma((steps,)),
            dma((chunks,)),
            dma((chunks,)),
            dma((chunks,)),
            dma((chunks,)),
            dma((chunks,)),
            dma((chunks,)),
            dma(()),
        ],
        compiler_params=pltpu.CompilerParams(
            collective_id=1, has_side_effects=True, vmem_limit_bytes=VMEM_LIMIT
        ),
    )(
        long_blocks, queries, keys, values, attn_grad, out_weight, lin_out, sparse_out, state,
        dq_sp, dk_sp, dv_sp, pairs,
    )


def solution(mesh):
    return jax.shard_map(
        local,
        mesh=mesh,
        in_specs=(
            P("ctx", "head"),
            P("ctx", "head"),
            P("ctx", "head"),
            P(None, "head"),
            P("ctx", "head"),
            P(),
        ),
        out_specs=(P("ctx", "head"), P("ctx", "head"), P("ctx", "head"), P("ctx", "head")),
        check_vma=False,
    )
```

```python
import functools
import math

import jax
import jax.numpy as jnp
from jax import lax
from jax.experimental import pallas as pl
from jax.experimental.pallas import tpu as pltpu
from jax.sharding import PartitionSpec as P

HD = 128
LIN_DEV = 3
LISTED = 4
BLOCK = 512
CHUNK = 256
SCALING = 1.0 / math.sqrt(HD)
MESH = pl.DeviceIdType.MESH
VMEM_LIMIT = 56 * 1024 * 1024


def mm(a, b):
    return jnp.dot(a, b, preferred_element_type=jnp.float32)


def mm_nt(a, b):
    return lax.dot_general(a, b, (((1,), (1,)), ((), ())), preferred_element_type=jnp.float32)


def mm_tn(a, b):
    return lax.dot_general(a, b, (((0,), (0,)), ((), ())), preferred_element_type=jnp.float32)


def bf16(x):
    return x.astype(jnp.bfloat16)


def block_scale(ctx_place, row_count, b):
    first = ctx_place * row_count + b * BLOCK
    rows = lax.broadcasted_iota(jnp.int32, (BLOCK, HD), 0) + (first + 1)
    scale = 1.0 / (math.sqrt(HD) * jnp.sqrt(rows.astype(jnp.float32)))
    return scale


def causal_mask():
    u = lax.broadcasted_iota(jnp.int32, (BLOCK, BLOCK), 0)
    s = lax.broadcasted_iota(jnp.int32, (BLOCK, BLOCK), 1)
    return u >= s


def remote(src, dst, send, recv, target):
    return pltpu.make_async_remote_copy(
        src_ref=src, dst_ref=dst, send_sem=send, recv_sem=recv, device_id=target, device_id_type=MESH
    )


def enter(n_ctx, me, sib, par):
    barrier = pltpu.get_barrier_semaphore()
    for other in (sib, par):
        pl.semaphore_signal(barrier, inc=1, device_id={"head": other}, device_id_type=MESH)

    def greet(s, carry):
        to = lax.rem(me + s, n_ctx)
        pl.semaphore_signal(barrier, inc=1, device_id={"ctx": to}, device_id_type=MESH)
        return carry

    lax.fori_loop(1, n_ctx, greet, 0)
    pl.semaphore_wait(barrier, n_ctx + 1)


def asked(table, place, block, nblocks):
    count = jnp.int32(0)
    for i in range(nblocks):
        for r in range(LISTED):
            count = count + (table[place * nblocks + i, r] == block).astype(jnp.int32)
    return count


class Scan:
    def __init__(self, n_ctx, me, backward, own, total, out, arrived, send, recv):
        self.n_ctx, self.me, self.backward = n_ctx, me, backward
        self.own, self.total, self.out, self.arrived = own, total, out, arrived
        self.send, self.recv = send, recv
        self.steps = (n_ctx - 1).bit_length()

    def copy(self, i):
        shift = self.n_ctx - (1 << i) if self.backward else 1 << i
        to = lax.rem(self.me + shift, self.n_ctx)
        return remote(self.out.at[i], self.arrived.at[i], self.send.at[i], self.recv.at[i], {"ctx": to})

    def sends(self, i):
        return self.me >= (1 << i) if self.backward else self.me < self.n_ctx - (1 << i)

    def receives(self, i):
        return self.me < self.n_ctx - (1 << i) if self.backward else self.me >= (1 << i)

    def begin(self):
        self.total[...] = jnp.zeros_like(self.total)
        self.start(0)

    def start(self, i):
        self.out[i] = bf16(self.own[...] + self.total[...])

        @pl.when(self.sends(i))
        def _():
            self.copy(i).start()

    def receive(self, i):
        @pl.when(self.receives(i))
        def _():
            self.copy(i).wait_recv()
            self.total[...] += self.arrived[i].astype(jnp.float32)

    def advance(self, i):
        if i < self.steps:
            self.receive(i)
            if i + 1 < self.steps:
                self.start(i + 1)

    def finish(self):
        for i in range(self.steps):
            @pl.when(self.sends(i))
            def _():
                self.copy(i).wait_send()


def gather_kernel(
    n_ctx, table, q, k, v, og, w,
    g_out, lin_out, state_out, kv_in,
    og_sib, og_par, og_far, kv_out, lin_acc, st_blk, st_own, st_sum, st_out, st_in, total,
    sib_sems, par_send, par_recv, far_send, far_recv, kv_send, kv_recv, st_send, st_recv, own_sem,
):
    me = lax.axis_index("ctx")
    h = lax.axis_index("head")
    sib = h + 1 - 2 * lax.rem(h, 2)
    par = lax.rem(h + 2, 4)
    far = lax.rem(sib + 2, 4)
    rows, width = og.shape
    nblocks = rows // BLOCK
    chunks = rows // CHUNK
    enter(n_ctx, me, sib, par)

    def part(c):
        return pl.ds(pl.multiple_of(c * CHUNK, CHUNK), CHUNK)

    def par_copy(c):
        return remote(og.at[part(c)], og_par.at[part(c)], par_send.at[c], par_recv.at[c], {"head": par})

    def far_copy(c):
        return remote(og_par.at[part(c)], og_far.at[part(c)], far_send.at[c], far_recv.at[c], {"head": sib})

    sib_copy = remote(og, og_sib, sib_sems.at[0], sib_sems.at[1], {"head": sib})

    def kv_copy(s):
        to = lax.rem(me + s, n_ctx)
        return remote(kv_out.at[s], kv_in.at[me], kv_send.at[s], kv_recv.at[s], {"ctx": to})

    scan = Scan(n_ctx, me, False, st_own, st_sum, st_out, st_in, st_send, st_recv)

    def loop(first, last, step):
        def body(i, carry):
            step(i)
            return carry

        lax.fori_loop(first, last, body, 0)

    loop(0, chunks, lambda c: par_copy(c).start())

    def fill(s):
        to = lax.rem(me + s, n_ctx)
        picked_k = jnp.zeros((BLOCK, HD), jnp.float32)
        picked_v = jnp.zeros((BLOCK, HD), jnp.float32)
        for b in range(nblocks):
            here = slice(b * BLOCK, (b + 1) * BLOCK)
            chosen = asked(table, to, me * nblocks + b, nblocks).astype(jnp.float32)
            picked_k = picked_k + chosen * k[here, LIN_DEV * HD:].astype(jnp.float32)
            picked_v = picked_v + chosen * v[here, LIN_DEV * HD:].astype(jnp.float32)
        kv_out[s, :, :HD] = bf16(picked_k)
        kv_out[s, :, HD:] = bf16(picked_v)

    def fill_send(s):
        fill(s)
        kv_copy(s).start()

    for head in range(LIN_DEV):
        cols = slice(head * HD, (head + 1) * HD)
        device_state = jnp.zeros((HD, HD), jnp.float32)
        for b in range(nblocks):
            here = slice(b * BLOCK, (b + 1) * BLOCK)
            state = mm_tn(k[here, cols], v[here, cols])
            st_blk[b, head] = state
            device_state = device_state + state
        st_own[head] = device_state
    scan.begin()
    loop(1, n_ctx, fill_send)
    sib_copy.start()
    fill(0)
    own_copy = pltpu.make_async_copy(kv_out.at[0], kv_in.at[me], own_sem)
    own_copy.start()

    own_rows = pl.ds(pl.multiple_of(h * width, width), width)

    def own_product(c):
        total[part(c)] = mm(og[part(c)], w[own_rows])

    loop(0, chunks, own_product)
    scan.advance(0)
    sib_rows = pl.ds(pl.multiple_of(sib * width, width), width)
    sib_copy.wait_recv()

    def sib_product(c):
        total[part(c)] += mm(og_sib[part(c)], w[sib_rows])

    loop(0, chunks, sib_product)
    for b in range(nblocks):
        scale = block_scale(me, rows, b)
        here = slice(b * BLOCK, (b + 1) * BLOCK)
        for head in range(LIN_DEV):
            cols = slice(head * HD, (head + 1) * HD)
            scores = mm_nt(q[here, cols], k[here, cols])
            weights = bf16(jnp.where(causal_mask(), scale[:, :1] * scores, 0.0))
            inside = mm(weights, v[here, cols])
            lin_acc[here, cols] = inside

    par_rows = pl.ds(pl.multiple_of(par * width, width), width)
    far_rows = pl.ds(pl.multiple_of(far * width, width), width)

    def forward(c):
        par_copy(c).wait_recv()
        far_copy(c).start()
        total[part(c)] += mm(og_par[part(c)], w[par_rows])

    loop(0, chunks // 2, forward)
    scan.advance(1)
    loop(chunks // 2, chunks, forward)
    for i in range(2, scan.steps):
        scan.advance(i)
    for head in range(LIN_DEV):
        state = st_sum[head]
        for b in range(nblocks):
            state_out[b, head] = bf16(state)
            state = state + st_blk[b, head]

    for b in range(nblocks):
        scale = block_scale(me, rows, b)
        here = slice(b * BLOCK, (b + 1) * BLOCK)
        for head in range(LIN_DEV):
            cols = slice(head * HD, (head + 1) * HD)
            across = mm(q[here, cols], state_out[b, head])
            lin_out[here, cols] = bf16(lin_acc[here, cols] + scale * across)


    def last(c):
        far_copy(c).wait_recv()
        g_out[part(c)] = bf16(total[part(c)] + mm(og_far[part(c)], w[far_rows]))

    loop(0, chunks, last)

    loop(1, n_ctx, lambda s: kv_copy(s).wait())
    scan.finish()

    def finish_chunk(c):
        par_copy(c).wait_send()
        far_copy(c).wait_send()

    loop(0, chunks, finish_chunk)
    sib_copy.wait_send()
    own_copy.wait()


def sparse_kernel(
    table, place, q, k, v, g, far0, far1, far2, far3,
    out, dq_out, dk_out, dv_out, pairs,
    probs, pair_buf, sems,
):
    b = pl.program_id(0)
    nblocks = pl.num_programs(0)
    here = place[0] * nblocks + b
    fars = (far0, far1, far2, far3)
    neg = jnp.float32(-jnp.inf)
    qb, kb, vb, gb = q[...], k[...], v[...], g[...]
    scores = jnp.where(causal_mask(), mm_nt(qb, kb), neg)
    probs[0] = scores
    peak = jnp.max(scores, axis=1, keepdims=True)
    for r in range(LISTED):
        bias = jnp.where(table[here, r] != here, jnp.float32(0.0), neg)
        scores = mm_nt(qb, fars[r][0, :, :HD]) + bias
        probs[r + 1] = scores
        peak = jnp.maximum(peak, jnp.max(scores, axis=1, keepdims=True))
    sums = jnp.zeros((BLOCK, 1), jnp.float32)
    for r in range(LISTED + 1):
        e = jnp.exp((probs[r] - peak) * SCALING)
        probs[r] = e
        sums = sums + jnp.sum(e, axis=1, keepdims=True)
    inv = 1.0 / sums
    result = jnp.zeros((BLOCK, HD), jnp.float32)
    for r in range(LISTED + 1):
        prob = probs[r] * inv
        probs[r] = prob
        weight = bf16(prob)
        val = vb if r == 0 else fars[r - 1][0, :, HD:]
        result = result + mm(weight, val)
        dv = mm_tn(weight, gb)
        if r == 0:
            dv_out[...] = dv
        else:
            pair_buf[r - 1, :, HD:] = bf16(dv)
    result = bf16(result)
    out[...] = result
    row_dot = jnp.sum(gb.astype(jnp.float32) * result.astype(jnp.float32), axis=1, keepdims=True)
    dq = jnp.zeros((BLOCK, HD), jnp.float32)
    for r in range(LISTED + 1):
        val = vb if r == 0 else fars[r - 1][0, :, HD:]
        key = kb if r == 0 else fars[r - 1][0, :, :HD]
        ds = bf16(probs[r] * (mm_nt(gb, val) - row_dot))
        dq = dq + mm(ds, key)
        dk = SCALING * mm_tn(ds, qb)
        if r == 0:
            dk_out[...] = dk
        else:
            pair_buf[r - 1, :, :HD] = bf16(dk)
    dq_out[...] = bf16(SCALING * dq)
    copies = [
        pltpu.make_async_copy(pair_buf.at[r], pairs.at[table[here, r] // nblocks], sems.at[r]) for r in range(LISTED)
    ]
    for copy in copies:
        copy.start()
    for copy in copies:
        copy.wait()


def scatter_kernel(
    n_ctx, table, q, k, v, g, w, lin, sp, state, dq_sp, dk_sp, dv_sp, pairs,
    layer, dq_out, dk_out, dv_out,
    ret, att, to_far, from_far, to_par, from_par, to_sib, from_sib, own, dk_acc, dv_acc, adj_blk, adj_own, adj_sum, adj_out, adj_in, adj,
    ret_send, ret_recv, adj_send, adj_recv, far_send, far_recv, par_send, par_recv, sib_send, sib_recv, own_sem,
):
    me = lax.axis_index("ctx")
    h = lax.axis_index("head")
    sib = h + 1 - 2 * lax.rem(h, 2)
    par = lax.rem(h + 2, 4)
    far = lax.rem(sib + 2, 4)
    rows, width = own.shape
    nblocks = rows // BLOCK
    chunks = rows // CHUNK
    enter(n_ctx, me, sib, par)

    def part(c):
        return pl.ds(pl.multiple_of(c * CHUNK, CHUNK), CHUNK)

    def loop(first, last, step):
        def body(i, carry):
            step(i)
            return carry

        lax.fori_loop(first, last, body, 0)

    def ret_copy(s):
        to = lax.rem(me + s, n_ctx)
        return remote(pairs.at[to], ret.at[me], ret_send.at[s], ret_recv.at[s], {"ctx": to})

    scan = Scan(n_ctx, me, True, adj_own, adj_sum, adj_out, adj_in, adj_send, adj_recv)

    def far_copy(c):
        return remote(to_far.at[part(c)], from_far.at[part(c)], far_send.at[c], far_recv.at[c], {"head": sib})

    def par_copy(c):
        return remote(to_par.at[part(c)], from_par.at[part(c)], par_send.at[c], par_recv.at[c], {"head": par})

    def sib_copy(c):
        return remote(to_sib.at[part(c)], from_sib.at[part(c)], sib_send.at[c], sib_recv.at[c], {"head": sib})

    for head in range(LIN_DEV):
        cols = slice(head * HD, (head + 1) * HD)
        device_adj = jnp.zeros((HD, HD), jnp.float32)
        for b in range(nblocks):
            here = slice(b * BLOCK, (b + 1) * BLOCK)
            scaled = bf16(block_scale(me, rows, b) * g[here, cols].astype(jnp.float32))
            one = mm_tn(q[here, cols], scaled)
            adj_blk[b, head] = one
            device_adj = device_adj + one
        adj_own[head] = device_adj
    scan.begin()
    loop(1, n_ctx, lambda s: ret_copy(s).start())
    own_copy = pltpu.make_async_copy(pairs.at[me], ret.at[me], own_sem)
    own_copy.start()
    att[:, :LIN_DEV * HD] = lin[...]
    att[:, LIN_DEV * HD:] = sp[...]

    def product(c, dest):
        return mm_nt(att[part(c)], w[pl.ds(pl.multiple_of(dest * width, width), width)])

    def far_step(c):
        to_far[part(c)] = bf16(product(c, far))
        far_copy(c).start()

    def par_step(c):
        mine = product(c, par)
        far_copy(c).wait_recv()
        to_par[part(c)] = bf16(mine + from_far[part(c)].astype(jnp.float32))
        par_copy(c).start()

    def both_step(c):
        far_step(c + 1)
        par_step(c)

    far_step(0)
    both_step(0)
    scan.advance(0)
    loop(1, chunks - 1, both_step)
    par_step(chunks - 1)
    scan.advance(1)

    def sib_step(c):
        to_sib[part(c)] = bf16(product(c, sib))
        sib_copy(c).start()

    loop(0, chunks, sib_step)

    def own_step(c):
        own[part(c)] = product(c, h)

    loop(0, chunks, own_step)

    for b in range(nblocks):
        scale = block_scale(me, rows, b)
        here = slice(b * BLOCK, (b + 1) * BLOCK)
        for head in range(LIN_DEV):
            cols = slice(head * HD, (head + 1) * HD)
            qb, kb, vb, gb = q[here, cols], k[here, cols], v[here, cols], g[here, cols]
            keep = causal_mask()
            weights = bf16(jnp.where(keep, scale[:, :1] * mm_nt(qb, kb), 0.0))
            grads = bf16(jnp.where(keep, scale[:, :1] * mm_nt(gb, vb), 0.0))
            dq_out[here, cols] = bf16(mm(grads, kb) + scale * mm_nt(gb, state[b, head]))
            dk_acc[here, cols] = mm_tn(grads, qb)
            dv_acc[here, cols] = mm_tn(weights, gb)
        dq_out[here, LIN_DEV * HD:] = dq_sp[here]

    own_copy.wait()
    loop(1, n_ctx, lambda s: ret_copy(s).wait())
    last = slice(LIN_DEV * HD, (LIN_DEV + 1) * HD)
    for b in range(nblocks):
        for t in range(BLOCK // HD):
            here = slice(t * HD, (t + 1) * HD)
            place = slice(b * BLOCK + t * HD, b * BLOCK + (t + 1) * HD)

            def add(j, sums):
                mine = jnp.full((1, 2 * HD), asked(table, j, me * nblocks + b, nblocks), jnp.int32) > 0
                got = ret[j, here].astype(jnp.float32)
                return sums + jnp.where(mine, got, 0.0)

            sums = lax.fori_loop(0, n_ctx, add, jnp.zeros((HD, 2 * HD), jnp.float32))
            dk_out[place, last] = bf16(dk_sp[place] + sums[:, :HD])
            dv_out[place, last] = bf16(dv_sp[place] + sums[:, HD:])

    def final(c):
        sib_copy(c).wait()
        par_copy(c).wait()
        far_copy(c).wait_send()
        layer[part(c)] = bf16(
            own[part(c)] + from_sib[part(c)].astype(jnp.float32) + from_par[part(c)].astype(jnp.float32)
        )

    loop(0, chunks, final)
    for i in range(2, scan.steps):
        scan.advance(i)
    for head in range(LIN_DEV):
        total = adj_sum[head]
        for b in reversed(range(nblocks)):
            adj[b, head] = bf16(total)
            total = total + adj_blk[b, head]

    for b in range(nblocks):
        here = slice(b * BLOCK, (b + 1) * BLOCK)
        for head in range(LIN_DEV):
            cols = slice(head * HD, (head + 1) * HD)
            dk_out[here, cols] = bf16(dk_acc[here, cols] + mm_nt(v[here, cols], adj[b, head]))
            dv_out[here, cols] = bf16(dv_acc[here, cols] + mm(k[here, cols], adj[b, head]))
    scan.finish()


def local(queries, keys, values, out_weight, out_grad, long_blocks):
    rows = queries.shape[0]
    nblocks = rows // BLOCK
    n_ctx = lax.axis_size("ctx")
    place = lax.axis_index("ctx").astype(jnp.int32).reshape(1)
    width = out_grad.shape[1]
    chunks = rows // CHUNK
    wide = LIN_DEV * HD
    steps = (n_ctx - 1).bit_length()

    smem = pl.BlockSpec(memory_space=pltpu.SMEM)
    vmem = pl.BlockSpec(memory_space=pltpu.VMEM)
    anywhere = pl.BlockSpec(memory_space=pl.ANY)
    b16, f32 = jnp.bfloat16, jnp.float32
    dma = pltpu.SemaphoreType.DMA

    attn_grad, lin_out, state, kv_in = pl.pallas_call(
        functools.partial(gather_kernel, n_ctx),
        name="gather",
        out_shape=(
            jax.ShapeDtypeStruct((rows, wide + HD), b16),
            jax.ShapeDtypeStruct((rows, wide), b16),
            jax.ShapeDtypeStruct((nblocks, LIN_DEV, HD, HD), b16),
            jax.ShapeDtypeStruct((n_ctx, BLOCK, 2 * HD), b16),
        ),
        in_specs=[smem] + [vmem] * 5,
        out_specs=(vmem, vmem, vmem, anywhere),
        scratch_shapes=[
            pltpu.VMEM((rows, width), b16),
            pltpu.VMEM((rows, width), b16),
            pltpu.VMEM((rows, width), b16),
            pltpu.VMEM((n_ctx, BLOCK, 2 * HD), b16),
            pltpu.VMEM((rows, wide), f32),
            pltpu.VMEM((nblocks, LIN_DEV, HD, HD), f32),
            pltpu.VMEM((LIN_DEV, HD, HD), f32),
            pltpu.VMEM((LIN_DEV, HD, HD), f32),
            pltpu.VMEM((steps, LIN_DEV, HD, HD), b16),
            pltpu.VMEM((steps, LIN_DEV, HD, HD), b16),
            pltpu.VMEM((rows, wide + HD), f32),
            dma((2,)),
            dma((chunks,)),
            dma((chunks,)),
            dma((chunks,)),
            dma((chunks,)),
            dma((n_ctx,)),
            dma((n_ctx,)),
            dma((steps,)),
            dma((steps,)),
            dma(()),
        ],
        compiler_params=pltpu.CompilerParams(
            collective_id=0, has_side_effects=True, vmem_limit_bytes=VMEM_LIMIT
        ),
    )(long_blocks, queries, keys, values, out_grad, out_weight)

    column = pl.BlockSpec((BLOCK, HD), lambda b, table, place: (b, LIN_DEV))
    single = pl.BlockSpec((BLOCK, HD), lambda b, table, place: (b, 0))

    def far_spec(r):
        return pl.BlockSpec((1, BLOCK, 2 * HD), lambda b, table, place: (table[place[0] * nblocks + b, r] // nblocks, 0, 0))

    sparse_out, dq_sp, dk_sp, dv_sp, pairs = pl.pallas_call(
        sparse_kernel,
        name="sparse",
        out_shape=(
            jax.ShapeDtypeStruct((rows, HD), b16),
            jax.ShapeDtypeStruct((rows, HD), b16),
            jax.ShapeDtypeStruct((rows, HD), f32),
            jax.ShapeDtypeStruct((rows, HD), f32),
            jax.ShapeDtypeStruct((n_ctx, BLOCK, 2 * HD), b16),
        ),
        grid_spec=pltpu.PrefetchScalarGridSpec(
            num_scalar_prefetch=2,
            grid=(nblocks,),
            in_specs=[column] * 4 + [far_spec(r) for r in range(LISTED)],
            out_specs=(single, single, single, single, anywhere),
            scratch_shapes=[
                pltpu.VMEM((LISTED + 1, BLOCK, BLOCK), f32),
                pltpu.VMEM((LISTED, BLOCK, 2 * HD), b16),
                dma((LISTED,)),
            ],
        ),
        compiler_params=pltpu.CompilerParams(vmem_limit_bytes=VMEM_LIMIT),
    )(long_blocks, place, queries, keys, values, attn_grad, kv_in, kv_in, kv_in, kv_in)

    big = pltpu.VMEM((rows, width), b16)
    return pl.pallas_call(
        functools.partial(scatter_kernel, n_ctx),
        name="scatter",
        out_shape=(
            jax.ShapeDtypeStruct((rows, width), b16),
            jax.ShapeDtypeStruct((rows, wide + HD), b16),
            jax.ShapeDtypeStruct((rows, wide + HD), b16),
            jax.ShapeDtypeStruct((rows, wide + HD), b16),
        ),
        in_specs=[smem] + [vmem] * 11 + [anywhere],
        out_specs=(vmem, vmem, vmem, vmem),
        scratch_shapes=[
            pltpu.VMEM((n_ctx, BLOCK, 2 * HD), b16),
            pltpu.VMEM((rows, wide + HD), b16),
            big, big, big, big, big, big,
            pltpu.VMEM((rows, width), f32),
            pltpu.VMEM((rows, wide), f32),
            pltpu.VMEM((rows, wide), f32),
            pltpu.VMEM((nblocks, LIN_DEV, HD, HD), f32),
            pltpu.VMEM((LIN_DEV, HD, HD), f32),
            pltpu.VMEM((LIN_DEV, HD, HD), f32),
            pltpu.VMEM((steps, LIN_DEV, HD, HD), b16),
            pltpu.VMEM((steps, LIN_DEV, HD, HD), b16),
            pltpu.VMEM((nblocks, LIN_DEV, HD, HD), b16),
            dma((n_ctx,)),
            dma((n_ctx,)),
            dma((steps,)),
            dma((steps,)),
            dma((chunks,)),
            dma((chunks,)),
            dma((chunks,)),
            dma((chunks,)),
            dma((chunks,)),
            dma((chunks,)),
            dma(()),
        ],
        compiler_params=pltpu.CompilerParams(
            collective_id=1, has_side_effects=True, vmem_limit_bytes=VMEM_LIMIT
        ),
    )(
        long_blocks, queries, keys, values, attn_grad, out_weight, lin_out, sparse_out, state,
        dq_sp, dk_sp, dv_sp, pairs,
    )


def solution(mesh):
    return jax.shard_map(
        local,
        mesh=mesh,
        in_specs=(
            P("ctx", "head"),
            P("ctx", "head"),
            P("ctx", "head"),
            P(None, "head"),
            P("ctx", "head"),
            P(),
        ),
        out_specs=(P("ctx", "head"), P("ctx", "head"), P("ctx", "head"), P("ctx", "head")),
        check_vma=False,
    )
```
